512 devices in a mesh: dp: 32 (over x_hi, y, core), mp: 16 (over x_lo, z).
Axes of the slice: x: 4 (x_hi: 2, x_lo: 2; x = x_hi * 2 + x_lo), y: 8, z: 8, core: 2. Of those that a mesh axis runs over, the one named last changes fastest.
Arguments:
- tokens: bfloat16 [8192, 3072], P('dp'), may hold values from -6 to 6
- layer_norm_gain: float32 [3072], replicated, may hold values from 0.5 to 1.5
- w_up: bfloat16 [3072, 12288], P(None, 'mp'), may hold values from -0.109375 to 0.109375
- w_down: bfloat16 [12288, 3072], P('mp'), may hold values from -0.078125 to 0.078125
- cotangent: bfloat16 [8192, 3072], P(('dp', 'mp')), may hold values from -6 to 6
Outputs:
- mixed: bfloat16 [8192, 3072], P(('dp', 'mp'))
- grad_tokens: bfloat16 [8192, 3072], P(('dp', 'mp'))
- grad_up: bfloat16 [3072, 12288], P(None, 'mp')
- grad_down: bfloat16 [12288, 3072], P('mp')
- gradient_of_gain: float32 [3072], replicated
The draws below stay inside these ranges and needn't reach their ends.
All inputs are finite; a program needn't handle non-finite values.
Results may differ from the reference program's by a relative error of at most 0.03.
Values may be sent and summed in bfloat16 or wider, within the bound.
A program may use at most 128 MiB of HBM per device.

```python
import math
import jax
import jax.numpy as jnp
from jax import lax

D = 3072
FF_DEV = 768
GROUP_TOK = 256
FF = 12288
TOKENS = 8192
N_DP = 32
N_MP = 16


def block_scale(stream_key, shape, shards, low, top_value):
    def one(axis_at, shards_of):
        draws = jax.random.uniform(jax.random.fold_in(jax.random.fold_in(stream_key, 6), axis_at), (shards_of,), jnp.float32, low / len(shards), top_value / len(shards))
        return jnp.repeat(jnp.exp(draws), shape[axis_at] // shards_of).reshape((-1,) + (1,) * (len(shape) - axis_at - 1))

    loudness = one(*shards[0])
    for cut in shards[1:]:
        loudness = loudness * one(*cut)
    return loudness


def gaussian(stream_key, extent, scale, limit, cuts=(), dtype=jnp.bfloat16):
    result = scale * jax.random.normal(stream_key, extent, jnp.float32)
    if cuts:
        result = result * block_scale(stream_key, extent, cuts, -0.22, 0.18)
    return jnp.clip(result, -limit, limit).astype(dtype)


def setup_inputs(seed: int = 0) -> dict:
    splits = jax.random.split(jax.random.key(seed), 6)
    tokens = gaussian(splits[0], (TOKENS, D), 1.0, 6.0, ((0, 32),))
    layer_norm_gain = jnp.clip(jax.random.uniform(splits[1], (D,), jnp.float32, 0.5, 1.5), 0.5, 1.5)
    w_up = gaussian(splits[2], (D, FF), D ** -0.5, 0.109375, ((1, 16),))
    w_down = gaussian(splits[3], (FF, D), (FF // 2) ** -0.5, 0.078125, ((0, 16),))
    cotangent = gaussian(splits[4], (TOKENS, D), 1.0, 6.0, ((0, 512),))
    return {"tokens": tokens, "layer_norm_gain": layer_norm_gain, "w_up": w_up, "w_down": w_down, "cotangent": cotangent}


def apply_layer_norm(tokens):
    values = tokens.astype(jnp.float32)
    centred = values - lax.optimization_barrier(jnp.mean(values, axis=1, keepdims=True))
    inverse_deviation = lax.rsqrt(lax.optimization_barrier(jnp.mean(centred * centred, axis=1, keepdims=True)) + 1e-06)
    return (centred * inverse_deviation, inverse_deviation)

def gelu_value(pre):
    return 0.5 * pre * (1.0 + jax.scipy.special.erf(pre / math.sqrt(2.0)))

def gelu_slope(pre):
    cumul = 0.5 * (1.0 + jax.scipy.special.erf(pre / math.sqrt(2.0)))
    density = jnp.exp(-0.5 * pre * pre) / math.sqrt(2.0 * math.pi)
    return cumul + pre * density

def rounded(value):
    return lax.optimization_barrier(value.astype(jnp.bfloat16)).astype(jnp.float32)

def hidden_blocks(left, right, width, blocks):

    def step(index, total):
        part_left = lax.dynamic_slice_in_dim(left, index * width, width, 1)
        part_right = lax.dynamic_slice_in_dim(right, index * width, width, 0)
        return total + rounded(jnp.dot(part_left, part_right, preferred_element_type=jnp.float32))
    start = jnp.zeros((left.shape[0], right.shape[1]), jnp.float32)
    return lax.fori_loop(0, blocks, step, start)

def group_blocks(left, right, height, groups):

    def step(index, total):
        part_left = lax.dynamic_slice_in_dim(left, index * height, height, 0)
        part_right = lax.dynamic_slice_in_dim(right, index * height, height, 0)
        return total + rounded(jnp.dot(part_left.T, part_right, preferred_element_type=jnp.float32))
    start = jnp.zeros((left.shape[1], right.shape[1]), jnp.float32)
    return lax.fori_loop(0, groups, step, start)

def reference(tokens, layer_norm_gain, w_up, w_down, cotangent):
    input_centred_hat, inverse_deviation = apply_layer_norm(tokens)
    normed_rows = (input_centred_hat * layer_norm_gain).astype(jnp.bfloat16)
    pre = jnp.dot(normed_rows, w_up, preferred_element_type=jnp.float32)
    act = gelu_value(pre).astype(jnp.bfloat16)
    branch = hidden_blocks(act, w_down, FF_DEV, N_MP)
    mixed = (tokens.astype(jnp.float32) + branch).astype(jnp.bfloat16)
    back_act = jnp.dot(cotangent, w_down.T, preferred_element_type=jnp.float32)
    grad_down = group_blocks(act, cotangent, GROUP_TOK, N_DP).astype(jnp.bfloat16)
    back_pre = (back_act * gelu_slope(pre)).astype(jnp.bfloat16)
    grad_up = group_blocks(normed_rows, back_pre, GROUP_TOK, N_DP).astype(jnp.bfloat16)
    backward_normed_rows = hidden_blocks(back_pre, w_up.T, FF_DEV, N_MP)
    gradient_of_gain = lax.optimization_barrier(jnp.sum(backward_normed_rows * input_centred_hat, axis=0))
    backward_centred_hat = backward_normed_rows * layer_norm_gain
    backward_input_rows = inverse_deviation * (backward_centred_hat - lax.optimization_barrier(jnp.mean(backward_centred_hat, axis=1, keepdims=True)) - input_centred_hat * lax.optimization_barrier(jnp.mean(backward_centred_hat * input_centred_hat, axis=1, keepdims=True)))
    grad_tokens = (cotangent.astype(jnp.float32) + backward_input_rows).astype(jnp.bfloat16)
    return (mixed, grad_tokens, grad_up, grad_down, gradient_of_gain)
```

```python
import math

import jax
import jax.numpy as jnp
from jax import lax
from jax.experimental import pallas as pl
from jax.experimental.pallas import tpu as pltpu
from jax.sharding import PartitionSpec as P

F32 = jnp.float32
BF16 = jnp.bfloat16
D = 3072
HALF = D // 2
FF = 768
ROWS = 256
NY = 8
NZ = 8
OWN = 16
UC, UB, UA = 192, 48, 96
DC, DB, DA = 96, 384, 768
U, DN = 0, 1
GAIN_ROUNDS = 9


def gelu_value(pre):
    return 0.5 * pre * (1.0 + lax.erf(pre * (1.0 / math.sqrt(2.0))))


def gelu_slope(pre):
    cumul = 0.5 * (1.0 + lax.erf(pre * (1.0 / math.sqrt(2.0))))
    density = jnp.exp(-0.5 * pre * pre) * (1.0 / math.sqrt(2.0 * math.pi))
    return cumul + pre * density


def dot_nn(a, b):
    return lax.dot_general(a, b, (((1,), (0,)), ((), ())), preferred_element_type=F32)


def dot_nt(a, b):
    return lax.dot_general(a, b, (((1,), (1,)), ((), ())), preferred_element_type=F32)


def mod8(v):
    return lax.rem(v + 16, 8)


def flip(v, b):
    return v + b - 2 * b * lax.rem(v // b, 2)


def kernel(
    tok_hbm, gain, wu_hbm, wd_hbm, cot_hbm,
    mixed, gtok, gup_hbm, gdn_hbm, ggain,
    tok, wu, wd, nrm, mean, inv, nT, nTs, cot, cot_sib, act, slope, aT, bp, brp, bnp,
    zrecv, zx, gu, gd, ru, rd, xu, xd, xau, xad, fu, fd, gacc, grecv,
    lsem, csem, crsem, xlsem, exs, exr, rs_s, rs_r, xs_s, xs_r, xa_s, xa_r,
    z_s, z_r, zx_s, zx_r, ag_s, ag_r, sb_s, sb_r, fx_s, fx_r, sx_s, sx_r, gn_s, gn_r,
):
    dp = lax.axis_index("dp")
    mp = lax.axis_index("mp")
    c = lax.rem(dp, 2)
    y = lax.rem(dp // 2, NY)
    xh = dp // 16
    z = lax.rem(mp, NZ)
    xl = mp // NZ

    def at_y(v):
        return (xh * 16 + v * 2 + c, mp)

    def at_z(v):
        return (dp, xl * NZ + v)

    sib = (dp + 1 - 2 * c, mp)
    xpart = (xh * -16 + 16 + y * 2 + c, mp)
    lpart = (dp, (1 - xl) * NZ + z)
    ydev = [at_y(mod8(y + 1)), at_y(mod8(y - 1))]
    zdev = [at_z(mod8(z + 1)), at_z(mod8(z - 1))]
    sign = [1, -1]

    def remote(src, dst, ssem, rsem, to):
        return pltpu.make_async_remote_copy(
            src_ref=src, dst_ref=dst, send_sem=ssem, recv_sem=rsem,
            device_id=to, device_id_type=pl.DeviceIdType.MESH,
        )

    load_cot = pltpu.make_async_copy(cot_hbm, cot.at[pl.ds(mp * OWN, OWN)], lsem.at[0])
    load_tok = pltpu.make_async_copy(tok_hbm, tok, lsem.at[1])
    load_wu = pltpu.make_async_copy(wu_hbm, wu, lsem.at[2])
    load_wd = pltpu.make_async_copy(wd_hbm, wd, lsem.at[3])
    for one in (load_cot, load_tok, load_wu, load_wd):
        one.start()
    barrier = pltpu.get_barrier_semaphore()
    greet = ydev + zdev + [
        sib, xpart, lpart, at_z(flip(z, 2)), at_z(flip(z, 4)), at_y(flip(y, 2)), at_y(flip(y, 4)),
    ]
    for one in greet:
        pl.semaphore_signal(barrier, inc=1, device_id=one, device_id_type=pl.DeviceIdType.MESH)
    pl.semaphore_wait(barrier, len(greet))

    def cot_rows(q, k):
        side = xl if q == 0 else 1 - xl
        return pl.ds(pl.multiple_of((side * NZ + k) * OWN, OWN), OWN)

    def cot_copy(q, j, d):
        rows = cot_rows(q, mod8(z - sign[d] * (j - 1)))
        ref = cot.at[rows] if j < 4 else cot.at[rows, pl.ds(d * HALF, HALF)]
        return remote(ref, ref, csem.at[q, j - 1, d], crsem.at[q, j - 1, d], zdev[d])

    def cot_arrival(q, j, d):
        rows = cot_rows(q, mod8(z - sign[d] * j))
        ref = cot.at[rows] if j < 4 else cot.at[rows, pl.ds(d * HALF, HALF)]
        return remote(ref, ref, csem.at[q, j - 1, d], crsem.at[q, j - 1, d], zdev[d])

    def cot_send(q, j):
        for d in range(2):
            cot_copy(q, j, d).start()

    def cot_wait(q, j):
        for d in range(2):
            cot_arrival(q, j, d).wait_recv()

    mine = cot.at[cot_rows(0, z)]
    theirs = cot.at[cot_rows(1, z)]
    load_cot.wait()
    cot_to_l = remote(mine, mine, xlsem.at[0], xlsem.at[1], lpart)
    cot_to_l.start()
    cot_send(0, 1)

    load_tok.wait()

    @pl.loop(0, ROWS // 32)
    def _(i):
        rows = pl.ds(pl.multiple_of(i * 32, 32), 32)
        v = tok[rows, :].astype(F32)
        mu = jnp.mean(v, axis=1, keepdims=True)
        cen = v - mu
        iv = lax.rsqrt(jnp.mean(cen * cen, axis=1, keepdims=True) + 1e-06)
        mean[rows, :] = mu
        inv[rows, :] = iv
        nrm[rows, :] = (cen * iv * gain[...]).astype(BF16)

    remote(theirs, theirs, xlsem.at[0], xlsem.at[1], lpart).wait_recv()
    cot_send(1, 1)
    cot_wait(0, 1)
    cot_send(0, 2)

    load_wu.wait()

    def pre_tile(t):
        cols = pl.ds(t * 256, 256)
        pre = dot_nn(nrm[...], wu[:, cols])
        a = gelu_value(pre)
        act[:, cols] = a.astype(BF16)
        slope[:, cols] = gelu_slope(pre)
        aT[cols, pl.ds(0, ROWS)] = a.T.astype(BF16)

    pre_tile(0)
    cot_wait(1, 1)
    cot_send(1, 2)
    cot_wait(0, 2)
    cot_send(0, 3)
    pre_tile(1)
    cot_wait(1, 2)
    cot_send(1, 3)
    cot_wait(0, 3)
    cot_send(0, 4)
    pre_tile(2)
    cot_wait(1, 3)
    cot_send(1, 4)

    mineK, theirsK = pl.ds(0, ROWS), pl.ds(ROWS, ROWS)
    act_x = remote(aT.at[:, mineK], aT.at[:, theirsK], exs.at[0], exr.at[0], sib)
    act_x.start()

    @pl.loop(0, HALF // 256)
    def _(j):
        rows = pl.ds(pl.multiple_of(j * 256, 256), 256)
        own = pl.ds(pl.multiple_of(c * HALF + j * 256, 256), 256)
        other = pl.ds(pl.multiple_of((1 - c) * HALF + j * 256, 256), 256)
        nT[rows, mineK] = nrm[:, own].astype(F32).T.astype(BF16)
        nTs[rows, :] = nrm[:, other].astype(F32).T.astype(BF16)

    nrm_x = remote(nTs, nT.at[:, theirsK], exs.at[1], exr.at[1], sib)
    nrm_x.start()

    load_wd.wait()

    @pl.loop(0, D // 512)
    def _(t):
        cols = pl.ds(pl.multiple_of(t * 512, 512), 512)
        brp[:, :, :, cols] = dot_nn(act[...], wd[:, cols]).astype(BF16).reshape(2, NZ, OWN, 512)

    for q in range(2):
        cot_wait(q, 4)

    ownC = pl.ds(pl.multiple_of(c * HALF, HALF), HALF)
    otherC = pl.ds(pl.multiple_of((1 - c) * HALF, HALF), HALF)
    cot_x = remote(cot.at[:, otherC], cot_sib, exs.at[2], exr.at[2], sib)
    cot_x.start()

    @pl.loop(0, FF // 256)
    def _(t):
        rows = pl.ds(pl.multiple_of(t * 256, 256), 256)
        back = dot_nt(cot[...], wd[rows, :])
        bp[mineK, rows] = (back * slope[:, rows]).astype(BF16)

    bp_x = remote(bp.at[mineK], bp.at[theirsK], exs.at[3], exr.at[3], sib)
    bp_x.start()

    def reg(kind, k, d, lo, n, base):
        if kind == U:
            return (pl.ds(pl.multiple_of(base + k * UC + lo, 16), n), pl.ds(d * 384, 384))
        return (pl.ds(pl.multiple_of(k * DC + d * 48, 16), 48), pl.ds(pl.multiple_of(base + lo, 128), n))

    unit = (UB, DB)
    ring_n = (UA + UB, DA + DB)

    def ring(kind, k, d, base=0):
        return reg(kind, k, d, xh * unit[kind], ring_n[kind], base)

    def part_a(kind, k, d, base=0):
        return reg(kind, k, d, unit[kind], 2 * unit[kind], base)

    def part_b(kind, k, d, side, base=0):
        return reg(kind, k, d, side * 3 * unit[kind], unit[kind], base)

    g = (gu, gd)
    rr = (ru, rd)
    xr = (xu, xd)
    xa = (xau, xad)
    f = (fu, fd)

    def rs_chunk(s, d):
        return mod8(y - sign[d] * (1 + s))

    def x_first(kind, s, d):
        k = rs_chunk(s, d)
        return remote(
            g[kind].at[part_b(kind, k, d, 1 - xh)], xr[kind].at[s, d],
            xs_s.at[kind, s, d], xs_r.at[kind, s, d], xpart,
        )

    def x_first_all(kind):
        @pl.loop(0, NY)
        def _(s):
            for d in range(2):
                x_first(kind, s, d).start()

    remote(aT.at[:, mineK], aT.at[:, theirsK], exs.at[0], exr.at[0], sib).wait_recv()
    remote(cot.at[:, otherC], cot_sib, exs.at[2], exr.at[2], sib).wait_recv()

    @pl.loop(0, HALF // 512)
    def _(t):
        cols = pl.ds(pl.multiple_of(t * 512, 512), 512)
        part = pl.ds(pl.multiple_of(c * HALF + t * 512, 512), 512)
        gd[:, cols] = (
            dot_nn(aT[:, mineK], cot[:, part]) + dot_nn(aT[:, theirsK], cot_sib[:, cols])
        ).astype(BF16)

    x_first_all(DN)

    remote(nTs, nT.at[:, theirsK], exs.at[1], exr.at[1], sib).wait_recv()
    remote(bp.at[mineK], bp.at[theirsK], exs.at[3], exr.at[3], sib).wait_recv()

    @pl.loop(0, HALF // 512)
    def _(t):
        rows = pl.ds(pl.multiple_of(t * 512, 512), 512)
        gu[rows, :] = dot_nn(nT[rows, :], bp[...]).astype(BF16)

    x_first_all(U)

    def rs_copy(kind, s, d):
        k = rs_chunk(s, d)
        return remote(
            g[kind].at[ring(kind, k, d)], rr[kind].at[s, d], rs_s.at[kind, s, d], rs_r.at[kind, s, d], ydev[d],
        )

    def rs_step(s, first, last):
        for kind in (DN, U):
            for d in range(2):
                k = rs_chunk(s, d)
                x_first(kind, s, d).wait_recv()
                b = part_b(kind, k, d, xh)
                g[kind][b] = (g[kind][b].astype(F32) + xr[kind][s, d].astype(F32)).astype(BF16)
                if not first:
                    rs_copy(kind, s - 1, d).wait_recv()
                    r = ring(kind, k, d)
                    g[kind][r] = (g[kind][r].astype(F32) + rr[kind][s - 1, d].astype(F32)).astype(BF16)
                if not last:
                    rs_copy(kind, s, d).start()

    zp = (brp, bnp)

    def z_copy(kind, s, d):
        k = mod8(z - sign[d] * (1 + s))
        return remote(
            zp[kind].at[:, k, :, pl.ds(d * HALF, HALF)], zrecv.at[kind, s, d],
            z_s.at[kind, s, d], z_r.at[kind, s, d], zdev[d],
        )

    def z_step(s, first, last):
        for kind in range(2):
            for d in range(2):
                if not first:
                    z_copy(kind, s - 1, d).wait_recv()
                    k = mod8(z - sign[d] * (1 + s))
                    cols = pl.ds(d * HALF, HALF)
                    zp[kind][:, k, :, cols] = (
                        zp[kind][:, k, :, cols].astype(F32) + zrecv[kind, s - 1, d].astype(F32)
                    ).astype(BF16)
                if not last:
                    z_copy(kind, s, d).start()

    def gain_copy(r):
        to_dp, to_mp = dp, mp
        for n, (a, b) in enumerate(
            [
                at_z(flip(z, 1)), at_z(flip(z, 2)), at_z(flip(z, 4)),
                at_y(flip(y, 1)), at_y(flip(y, 2)), at_y(flip(y, 4)),
                lpart, xpart, sib,
            ]
        ):
            to_dp = jnp.where(r == n, a, to_dp)
            to_mp = jnp.where(r == n, b, to_mp)
        return remote(gacc.at[r], grecv.at[r], gn_s.at[r], gn_r.at[r], (to_dp, to_mp))

    def gain_finish(r):
        gain_copy(r).wait_recv()
        gacc[r + 1] = gacc[r] + grecv[r]

    rs_step(0, True, False)

    @pl.loop(0, D // 512)
    def _(t):
        cols = pl.ds(pl.multiple_of(t * 512, 512), 512)
        back = dot_nt(bp[mineK, :], wu[cols, :])
        bnp[:, :, :, cols] = back.astype(BF16).reshape(2, NZ, OWN, 512)
        hat = (tok[:, cols].astype(F32) - mean[...]) * inv[...]
        gacc[0, :, cols] = jnp.sum(back * hat, axis=0, keepdims=True)

    z_step(0, True, False)
    gain_copy(0).start()

    @pl.loop(1, 7)
    def _(s):
        rs_step(s, False, False)
        z_step(s, False, False)
        gain_finish(s - 1)
        gain_copy(s).start()

    rs_step(7, False, True)

    def a_copy(kind, d):
        return remote(
            g[kind].at[part_a(kind, y, d)], xa[kind].at[d], xa_s.at[kind, d], xa_r.at[kind, d], xpart,
        )

    for kind in (DN, U):
        for d in range(2):
            a_copy(kind, d).start()

    z_step(7, False, True)

    def zx_copy(kind):
        return remote(zp[kind].at[1 - xl, z], zx.at[kind], zx_s.at[kind], zx_r.at[kind], lpart)

    for kind in range(2):
        zx_copy(kind).start()
    gain_finish(6)
    gain_copy(7).start()

    def base(core):
        return core * HALF

    def ag_chunk(s, d):
        return mod8(y - sign[d] * s)

    def same(kind, r, ssem, rsem, to):
        return remote(f[kind].at[r], f[kind].at[r], ssem, rsem, to)

    def ag_copy(kind, s, d):
        return same(kind, ring(kind, ag_chunk(s, d), d, base(c)), ag_s.at[kind, s, d], ag_r.at[kind, s, d], ydev[d])

    def ag_arrival(kind, s, d):
        return same(kind, ring(kind, ag_chunk(s, d), d, base(c)), ag_s.at[kind, s - 1, d], ag_r.at[kind, s - 1, d], ydev[d])

    def sib_copy(kind, s, d, core):
        return same(kind, ring(kind, ag_chunk(s, d), d, base(core)), sb_s.at[kind, s, d], sb_r.at[kind, s, d], sib)

    def fx_copy(kind, s, d, side):
        return same(kind, part_b(kind, ag_chunk(s, d), d, side, base(c)), fx_s.at[kind, s, d], fx_r.at[kind, s, d], xpart)

    def sx_copy(kind, s, d, core):
        return same(kind, part_b(kind, ag_chunk(s, d), d, 1 - xh, base(core)), sx_s.at[kind, s, d], sx_r.at[kind, s, d], sib)

    for kind in (DN, U):
        for d in range(2):
            a_copy(kind, d).wait_recv()
            b, b_f = part_b(kind, y, d, xh), part_b(kind, y, d, xh, base(c))
            f[kind][b_f] = g[kind][b]
            a, a_f = part_a(kind, y, d), part_a(kind, y, d, base(c))
            f[kind][a_f] = (g[kind][a].astype(F32) + xa[kind][d].astype(F32)).astype(BF16)
            ag_copy(kind, 0, d).start()
            fx_copy(kind, 0, d, xh).start()
            sib_copy(kind, 0, d, c).start()

    rows = pl.ds(pl.multiple_of(mp * OWN, OWN), OWN)
    own_tok = tok[rows, :].astype(F32)
    for kind in range(2):
        zx_copy(kind).wait_recv()
    mixed[...] = (own_tok + (brp[xl, z].astype(F32) + zx[0].astype(F32))).astype(BF16)
    back_normed = bnp[xl, z].astype(F32) + zx[1].astype(F32)
    hat = (own_tok - mean[rows, :]) * inv[rows, :]
    back_hat = back_normed * gain[...]
    back_in = inv[rows, :] * (
        back_hat
        - jnp.mean(back_hat, axis=1, keepdims=True)
        - hat * jnp.mean(back_hat * hat, axis=1, keepdims=True)
    )
    gtok[...] = (cot[rows, :].astype(F32) + back_in).astype(BF16)

    def ag_step(s, last):
        for kind in (DN, U):
            for d in range(2):
                ag_arrival(kind, s, d).wait_recv()
                if not last:
                    ag_copy(kind, s, d).start()
                fx_copy(kind, s, d, xh).start()
                sib_copy(kind, s, d, c).start()
        for kind in (DN, U):
            for d in range(2):
                fx_copy(kind, s - 1, d, 1 - xh).wait_recv()
                sx_copy(kind, s - 1, d, c).start()

    @pl.loop(1, 7)
    def _(s):
        ag_step(s, False)

        @pl.when(s == 1)
        def _():
            gain_finish(7)
            gain_copy(8).start()

        @pl.when(s == 2)
        def _():
            gain_finish(8)

    ag_step(7, True)
    ggain[...] = gacc[GAIN_ROUNDS]
    for kind in (DN, U):
        for d in range(2):
            fx_copy(kind, 7, d, 1 - xh).wait_recv()
            sx_copy(kind, 7, d, c).start()

    @pl.loop(0, NY)
    def _(s):
        for kind in (DN, U):
            for d in range(2):
                sib_copy(kind, s, d, 1 - c).wait_recv()
                sx_copy(kind, s, d, 1 - c).wait_recv()

    out_u = pltpu.make_async_copy(fu, gup_hbm, lsem.at[4])
    out_d = pltpu.make_async_copy(fd, gdn_hbm, lsem.at[5])
    out_u.start()
    out_d.start()

    cot_to_l.wait_send()
    for q in range(2):
        for j in range(1, 5):
            for d in range(2):
                cot_copy(q, j, d).wait_send()
    for one in (act_x, nrm_x, cot_x, bp_x):
        one.wait_send()

    @pl.loop(0, NY)
    def _(s):
        for kind in range(2):
            for d in range(2):
                x_first(kind, s, d).wait_send()
                fx_copy(kind, s, d, xh).wait_send()
                sib_copy(kind, s, d, c).wait_send()
                sx_copy(kind, s, d, c).wait_send()

    @pl.loop(0, NY - 1)
    def _(s):
        for kind in range(2):
            for d in range(2):
                rs_copy(kind, s, d).wait_send()
                ag_copy(kind, s, d).wait_send()
                z_copy(kind, s, d).wait_send()

    for kind in range(2):
        zx_copy(kind).wait_send()
        for d in range(2):
            a_copy(kind, d).wait_send()

    @pl.loop(0, GAIN_ROUNDS)
    def _(r):
        gain_copy(r).wait_send()

    out_u.wait()
    out_d.wait()


def shards(tokens, layer_norm_gain, w_up, w_down, cotangent):
    anywhere = pl.BlockSpec(memory_space=pl.ANY)
    vmem = pl.BlockSpec(memory_space=pltpu.VMEM)
    dma = pltpu.SemaphoreType.DMA
    both = (2, NY, 2)
    mixed, grad_tokens, grad_up, grad_down, gain_grad = pl.pallas_call(
        kernel,
        out_shape=(
            jax.ShapeDtypeStruct((OWN, D), BF16),
            jax.ShapeDtypeStruct((OWN, D), BF16),
            jax.ShapeDtypeStruct((D, FF), BF16),
            jax.ShapeDtypeStruct((FF, D), BF16),
            jax.ShapeDtypeStruct((1, D), F32),
        ),
        in_specs=[anywhere, vmem, anywhere, anywhere, anywhere],
        out_specs=(vmem, vmem, anywhere, anywhere, vmem),
        scratch_shapes=[
            pltpu.VMEM((ROWS, D), BF16),
            pltpu.VMEM((D, FF), BF16),
            pltpu.VMEM((FF, D), BF16),
            pltpu.VMEM((ROWS, D), BF16),
            pltpu.VMEM((ROWS, 1), F32),
            pltpu.VMEM((ROWS, 1), F32),
            pltpu.VMEM((HALF, 2 * ROWS), BF16),
            pltpu.VMEM((HALF, ROWS), BF16),
            pltpu.VMEM((ROWS, D), BF16),
            pltpu.VMEM((ROWS, HALF), BF16),
            pltpu.VMEM((ROWS, FF), BF16),
            pltpu.VMEM((ROWS, FF), F32),
            pltpu.VMEM((FF, 2 * ROWS), BF16),
            pltpu.VMEM((2 * ROWS, FF), BF16),
            pltpu.VMEM((2, NZ, OWN, D), BF16),
            pltpu.VMEM((2, NZ, OWN, D), BF16),
            pltpu.VMEM((2, NZ - 1, 2, 2, OWN, HALF), BF16),
            pltpu.VMEM((2, OWN, D), BF16),
            pltpu.VMEM((HALF, FF), BF16),
            pltpu.VMEM((FF, HALF), BF16),
            pltpu.VMEM((NY - 1, 2, UA + UB, 384), BF16),
            pltpu.VMEM((NY - 1, 2, 48, DA + DB), BF16),
            pltpu.VMEM((NY, 2, UB, 384), BF16),
            pltpu.VMEM((NY, 2, 48, DB), BF16),
            pltpu.VMEM((2, UA, 384), BF16),
            pltpu.VMEM((2, 48, DA), BF16),
            pltpu.VMEM((D, FF), BF16),
            pltpu.VMEM((FF, D), BF16),
            pltpu.VMEM((GAIN_ROUNDS + 1, 1, D), F32),
            pltpu.VMEM((GAIN_ROUNDS, 1, D), F32),
            dma((6,)),
            dma((2, 4, 2)), dma((2, 4, 2)), dma((2,)),
            dma((4,)), dma((4,)),
            dma(both), dma(both), dma(both), dma(both),
            dma((2, 2)), dma((2, 2)),
            dma(both), dma(both), dma((2,)), dma((2,)),
            dma(both), dma(both), dma(both), dma(both),
            dma(both), dma(both), dma(both), dma(both),
            dma((GAIN_ROUNDS,)), dma((GAIN_ROUNDS,)),
        ],
        compiler_params=pltpu.CompilerParams(
            collective_id=0, has_side_effects=True, vmem_limit_bytes=58 * 2**20
        ),
        cost_estimate=pl.CostEstimate(
            flops=12 * ROWS * D * FF, bytes_accessed=22 * 2**20, transcendentals=2 * ROWS * FF
        ),
        name="mlp_block",
    )(tokens, layer_norm_gain.reshape(1, D), w_up, w_down, cotangent)
    return mixed, grad_tokens, grad_up, grad_down, gain_grad.reshape(D)


def solution(mesh):
    placed = (P("dp", None), P(), P(None, "mp"), P("mp", None), P(("dp", "mp"), None))
    return jax.shard_map(
        shards,
        mesh=mesh,
        in_specs=placed,
        out_specs=(P(("dp", "mp"), None), P(("dp", "mp"), None), P(None, "mp"), P("mp", None), P()),
        check_vma=False,
    )
```

```python
import math

import jax
import jax.numpy as jnp
from jax import lax
from jax.experimental import pallas as pl
from jax.experimental.pallas import tpu as pltpu
from jax.sharding import PartitionSpec as P

F32 = jnp.float32
BF16 = jnp.bfloat16
D = 3072
HALF = D // 2
FF = 768
ROWS = 256
NY = 8
NZ = 8
OWN = 16
UC, DC = 192, 96
UR, UW = 48, 384
U, DN = 0, 1
GAIN_ROUNDS = 6


def gelu_value(pre):
    return 0.5 * pre * (1.0 + lax.erf(pre * (1.0 / math.sqrt(2.0))))


def gelu_slope(pre):
    cumul = 0.5 * (1.0 + lax.erf(pre * (1.0 / math.sqrt(2.0))))
    density = jnp.exp(-0.5 * pre * pre) * (1.0 / math.sqrt(2.0 * math.pi))
    return cumul + pre * density


def dot_nn(a, b):
    return lax.dot_general(a, b, (((1,), (0,)), ((), ())), preferred_element_type=F32)


def dot_nt(a, b):
    return lax.dot_general(a, b, (((1,), (1,)), ((), ())), preferred_element_type=F32)


def mod8(v):
    return lax.rem(v + 16, 8)


def flip(v, b):
    return v + b - 2 * b * lax.rem(v // b, 2)


def kernel(
    tok_hbm, gain, wu_hbm, wd_hbm, cot_hbm,
    mixed, gtok, fu, fd, ggain,
    tok, wu, wd, nrm, mean, inv, nT, nTs, cot, cot_sib, act, slope, aT, bp, brp, bnp,
    zrecv, zx, gu, gd, rr, xr, xa, gz, gacc, grecv,
    lsem, sent, crsem, exr, rs_r, xs_r, xa_r, z_r, zx_r, ag_r, sib_r, fx_r, gz_r, gn_r,
):
    dp = lax.axis_index("dp")
    mp = lax.axis_index("mp")
    c = lax.rem(dp, 2)
    y = lax.rem(dp // 2, NY)
    xh = dp // 16
    z = lax.rem(mp, NZ)
    xl = mp // NZ

    s_cot, s_ex, s_rs, s_x1, s_xa, s_z, s_zx, s_ag, s_sib, s_fx, s_gz, s_gn = (sent.at[i] for i in range(12))

    def at_y(v):
        return (xh * 16 + v * 2 + c, mp)

    def at_z(v):
        return (dp, xl * NZ + v)

    sib = (dp + 1 - 2 * c, mp)
    xpart = (xh * -16 + 16 + y * 2 + c, mp)
    lpart = (dp, (1 - xl) * NZ + z)
    ydev = [at_y(mod8(y + 1)), at_y(mod8(y - 1))]
    zdev = [at_z(mod8(z + 1)), at_z(mod8(z - 1))]
    sign = [1, -1]

    def remote(src, dst, ssem, rsem, to):
        return pltpu.make_async_remote_copy(
            src_ref=src, dst_ref=dst, send_sem=ssem, recv_sem=rsem,
            device_id=to, device_id_type=pl.DeviceIdType.MESH,
        )

    load_cot = pltpu.make_async_copy(cot_hbm, cot.at[pl.ds(mp * OWN, OWN)], lsem.at[0])
    load_tok = pltpu.make_async_copy(tok_hbm, tok, lsem.at[1])
    load_wu = pltpu.make_async_copy(wu_hbm, wu, lsem.at[2])
    load_wd = pltpu.make_async_copy(wd_hbm, wd, lsem.at[3])
    for one in (load_cot, load_tok, load_wu, load_wd):
        one.start()
    barrier = pltpu.get_barrier_semaphore()
    zall = [at_z(mod8(z + j)) for j in range(1, NZ)]
    greet = ydev + zall + [sib, xpart, lpart, at_y(flip(y, 2)), at_y(flip(y, 4))]
    for one in greet:
        pl.semaphore_signal(barrier, inc=1, device_id=one, device_id_type=pl.DeviceIdType.MESH)
    pl.semaphore_wait(barrier, len(greet))

    def cot_rows(q, k):
        side = xl if q == 0 else 1 - xl
        return pl.ds(pl.multiple_of((side * NZ + k) * OWN, OWN), OWN)

    def cot_copy(q, j, d):
        rows = cot_rows(q, mod8(z - sign[d] * (j - 1)))
        ref = cot.at[rows] if j < 4 else cot.at[rows, pl.ds(d * HALF, HALF)]
        return remote(ref, ref, s_cot, crsem.at[q, j - 1, d], zdev[d])

    def cot_arrival(q, j, d):
        rows = cot_rows(q, mod8(z - sign[d] * j))
        ref = cot.at[rows] if j < 4 else cot.at[rows, pl.ds(d * HALF, HALF)]
        return remote(ref, ref, s_cot, crsem.at[q, j - 1, d], zdev[d])

    def cot_send(q, j):
        for d in range(2):
            cot_copy(q, j, d).start()

    def cot_wait(q, j):
        for d in range(2):
            cot_arrival(q, j, d).wait_recv()

    mine = cot.at[cot_rows(0, z)]
    theirs = cot.at[cot_rows(1, z)]
    load_cot.wait()
    cot_to_l = remote(mine, mine, s_cot, crsem.at[0, 4, 0], lpart)
    cot_to_l.start()
    cot_send(0, 1)

    load_tok.wait()

    def layer_norm(lo, hi):
        @pl.loop(lo // 32, hi // 32)
        def _(i):
            rows = pl.ds(pl.multiple_of(i * 32, 32), 32)
            v = tok[rows, :].astype(F32)
            mu = jnp.mean(v, axis=1, keepdims=True)
            cen = v - mu
            iv = lax.rsqrt(jnp.mean(cen * cen, axis=1, keepdims=True) + 1e-06)
            mean[rows, :] = mu
            inv[rows, :] = iv
            nrm[rows, :] = (cen * iv * gain[...]).astype(BF16)

    layer_norm(0, 128)
    remote(theirs, theirs, s_cot, crsem.at[0, 4, 0], lpart).wait_recv()
    cot_send(1, 1)
    layer_norm(128, 256)
    cot_wait(0, 1)
    cot_send(0, 2)

    load_wu.wait()

    def pre_tile(t):
        cols = pl.ds(t * 256, 256)
        pre = dot_nn(nrm[...], wu[:, cols])
        a = gelu_value(pre)
        act[:, cols] = a.astype(BF16)
        slope[:, cols] = gelu_slope(pre)
        aT[cols, pl.ds(0, ROWS)] = a.T.astype(BF16)

    mineK, theirsK = pl.ds(0, ROWS), pl.ds(ROWS, ROWS)
    act_x = remote(aT.at[:, mineK], aT.at[:, theirsK], s_ex, exr.at[0], sib)

    pre_tile(0)
    cot_wait(1, 1)
    cot_send(1, 2)
    pre_tile(1)
    cot_wait(0, 2)
    cot_send(0, 3)
    pre_tile(2)
    act_x.start()
    cot_wait(1, 2)
    cot_send(1, 3)

    @pl.loop(0, HALF // 256)
    def _(j):
        rows = pl.ds(pl.multiple_of(j * 256, 256), 256)
        own = pl.ds(pl.multiple_of(c * HALF + j * 256, 256), 256)
        other = pl.ds(pl.multiple_of((1 - c) * HALF + j * 256, 256), 256)
        nT[rows, mineK] = nrm[:, own].astype(F32).T.astype(BF16)
        nTs[rows, :] = nrm[:, other].astype(F32).T.astype(BF16)

    nrm_x = remote(nTs, nT.at[:, theirsK], s_ex, exr.at[1], sib)
    nrm_x.start()

    load_wd.wait()
    cot_wait(0, 3)
    cot_send(0, 4)

    @pl.loop(0, D // 512)
    def _(t):
        cols = pl.ds(pl.multiple_of(t * 512, 512), 512)
        brp[:, :, :, cols] = dot_nn(act[...], wd[:, cols]).astype(BF16).reshape(2, NZ, OWN, 512)

    cot_wait(1, 3)
    cot_send(1, 4)
    for q in range(2):
        cot_wait(q, 4)

    ownC = pl.ds(pl.multiple_of(c * HALF, HALF), HALF)
    otherC = pl.ds(pl.multiple_of((1 - c) * HALF, HALF), HALF)
    cot_x = remote(cot.at[:, otherC], cot_sib, s_ex, exr.at[2], sib)
    cot_x.start()

    zp = (brp, bnp)

    def z_cols(s, d):
        return (slice(None), mod8(z - sign[d] * (1 + s)), slice(None), pl.ds(d * HALF, HALF))

    def z_copy(kind, s, d):
        return remote(
            zp[kind].at[z_cols(s, d)], zrecv.at[kind, s, d], s_z, z_r.at[kind, s, d], zdev[d],
        )

    def z_step(kind, s, first=False, last=False):
        for d in range(2):
            if not first:
                z_copy(kind, s - 1, d).wait_recv()
                zp[kind][z_cols(s, d)] = (
                    zp[kind][z_cols(s, d)].astype(F32) + zrecv[kind, s - 1, d].astype(F32)
                ).astype(BF16)
            if not last:
                z_copy(kind, s, d).start()

    def zx_copy(kind):
        return remote(zp[kind].at[1 - xl, z], zx.at[kind], s_zx, zx_r.at[kind], lpart)

    z_step(0, 0, first=True)

    @pl.loop(0, FF // 256)
    def _(t):
        rows = pl.ds(pl.multiple_of(t * 256, 256), 256)
        back = dot_nt(cot[...], wd[rows, :])
        bp[mineK, rows] = (back * slope[:, rows]).astype(BF16)

    bp_x = remote(bp.at[mineK], bp.at[theirsK], s_ex, exr.at[3], sib)
    bp_x.start()
    z_step(0, 1)

    def unit(kind, k, d, u, n=1, base=0):
        if kind == U:
            return (pl.ds(pl.multiple_of(base + k * UC + u * UR, 16), n * UR), pl.ds(d * UW, UW))
        return (pl.ds(pl.multiple_of(k * DC + d * UR, 16), UR), pl.ds(pl.multiple_of(base + u * UW, 128), n * UW))

    g = (gu, gd)
    f = (fu, fd)
    kinds = (DN, U)
    mine_u = (1, 2, 3 * xh)

    def rs_chunk(s, d):
        return mod8(y - sign[d] * (1 + s))

    def x_first(kind, s, d):
        return remote(
            g[kind].at[unit(kind, rs_chunk(s, d), d, 3 - 3 * xh)], xr.at[kind, s, d],
            s_x1, xs_r.at[kind, s, d], xpart,
        )

    def x_first_start(kind, s):
        for d in range(2):
            x_first(kind, s, d).start()

    remote(aT.at[:, mineK], aT.at[:, theirsK], s_ex, exr.at[0], sib).wait_recv()
    remote(cot.at[:, otherC], cot_sib, s_ex, exr.at[2], sib).wait_recv()

    @pl.loop(0, HALF // 512)
    def _(t):
        cols = pl.ds(pl.multiple_of(t * 512, 512), 512)
        part = pl.ds(pl.multiple_of(c * HALF + t * 512, 512), 512)
        gd[:, cols] = (
            dot_nn(aT[:, mineK], cot[:, part]) + dot_nn(aT[:, theirsK], cot_sib[:, cols])
        ).astype(BF16)

    x_first_start(DN, 0)
    x_first_start(DN, 1)
    z_step(0, 2)

    remote(nTs, nT.at[:, theirsK], s_ex, exr.at[1], sib).wait_recv()
    remote(bp.at[mineK], bp.at[theirsK], s_ex, exr.at[3], sib).wait_recv()

    @pl.loop(0, HALF // 512)
    def _(t):
        rows = pl.ds(pl.multiple_of(t * 512, 512), 512)
        gu[rows, :] = dot_nn(nT[rows, :], bp[...]).astype(BF16)

    x_first_start(U, 0)
    x_first_start(U, 1)
    z_step(0, 3)

    def rs_copy(kind, s, d, p):
        return remote(
            g[kind].at[unit(kind, rs_chunk(s, d), d, mine_u[p])], rr.at[kind, s, d, p],
            s_rs, rs_r.at[kind, s, d, p], ydev[d],
        )

    def rs_step(kind, s, first=False, last=False):
        for p in range(3):
            for d in range(2):
                at = unit(kind, rs_chunk(s, d), d, mine_u[p])
                if p == 2:
                    x_first(kind, s, d).wait_recv()
                if not first:
                    rs_copy(kind, s - 1, d, p).wait_recv()
                if p == 2 or not first:
                    total = g[kind][at].astype(F32)
                    if p == 2:
                        total = total + xr[kind, s, d].astype(F32)
                    if not first:
                        total = total + rr[kind, s - 1, d, p].astype(F32)
                    g[kind][at] = total.astype(BF16)
                if not last:
                    rs_copy(kind, s, d, p).start()

    partners = [at_y(flip(y, 1)), at_y(flip(y, 2)), at_y(flip(y, 4)), lpart, xpart, sib]

    def gz_copy(j):
        return remote(gz.at[z], gz.at[z], s_gz, gz_r.at[0], zall[j - 1])

    def gain_copy(r):
        return remote(gacc.at[r], grecv.at[r], s_gn, gn_r.at[r], partners[r])

    def gain_z_finish():
        seven = gz.at[pl.ds(0, NZ - 1)]
        remote(seven, seven, s_gz, gz_r.at[0], sib).wait_recv()
        total = gz[0]
        for k in range(1, NZ):
            total = total + gz[k]
        gacc[0] = total
        gain_copy(0).start()

    def gain_finish(r):
        gain_copy(r).wait_recv()
        gacc[r + 1] = gacc[r] + grecv[r]
        if r + 1 < GAIN_ROUNDS:
            gain_copy(r + 1).start()

    rs_step(DN, 0, first=True)
    x_first_start(DN, 2)

    @pl.loop(0, D // 512)
    def _(t):
        cols = pl.ds(pl.multiple_of(t * 512, 512), 512)
        back = dot_nt(bp[mineK, :], wu[cols, :])
        bnp[:, :, :, cols] = back.astype(BF16).reshape(2, NZ, OWN, 512)
        hat = (tok[:, cols].astype(F32) - mean[...]) * inv[...]
        gz[z, :, cols] = jnp.sum(back * hat, axis=0, keepdims=True)

    rs_step(U, 0, first=True)
    x_first_start(U, 2)
    z_step(0, 4)
    z_step(1, 0, first=True)
    for j in range(1, NZ):
        gz_copy(j).start()

    @pl.loop(1, 7)
    def _(s):
        for kind in kinds:
            rs_step(kind, s)

            @pl.when(s < 6)
            def _():
                x_first_start(kind, s + 2)

        @pl.when(s < 3)
        def _():
            z_step(0, s + 4)

        @pl.when(s == 3)
        def _():
            z_step(0, 7, last=True)
            zx_copy(0).start()

        @pl.when(s > 3)
        def _():
            z_step(1, s - 3)

        @pl.when(s == 3)
        def _():
            gain_z_finish()

        @pl.when(s == 5)
        def _():
            gain_finish(0)

    def a_copy(kind, d, p):
        return remote(
            g[kind].at[unit(kind, y, d, mine_u[p])], xa.at[kind, d, p], s_xa, xa_r.at[kind, d, p], xpart,
        )

    def ag_chunk(s, d):
        return mod8(y - sign[d] * s)

    def same(kind, at, ssem, rsem, to):
        return remote(f[kind].at[at], f[kind].at[at], ssem, rsem, to)

    def out_unit(kind, s, d, u, n=1, core=c):
        return unit(kind, ag_chunk(s, d), d, u, n, core * HALF)

    def ag_copy(kind, s, d, p):
        return same(kind, out_unit(kind, s, d, mine_u[p]), s_ag, ag_r.at[kind, s, d, p], ydev[d])

    def ag_arrival(kind, s, d, p):
        return same(kind, out_unit(kind, s, d, mine_u[p]), s_ag, ag_r.at[kind, s - 1, d, p], ydev[d])

    def sa_copy(kind, s, d, core=c):
        return same(kind, out_unit(kind, s, d, 1, 2, core), s_sib, sib_r.at[0], sib)

    def sb_copy(kind, s, d, core=c):
        return same(kind, out_unit(kind, s, d, 3 * xh, 1, core), s_sib, sib_r.at[0], sib)

    def fx_copy(kind, s, d, side=xh):
        return same(kind, out_unit(kind, s, d, 3 * side), s_fx, fx_r.at[kind, s, d], xpart)

    def sx_copy(kind, s, d, core=c):
        return same(kind, out_unit(kind, s, d, 3 - 3 * xh, 1, core), s_sib, sib_r.at[0], sib)

    def x_arrived(s):
        for kind in kinds:
            for d in range(2):
                fx_copy(kind, s, d, 1 - xh).wait_recv()
                sx_copy(kind, s, d).start()

    def ag_a(s, send=True):
        for kind in kinds:
            for p in range(2):
                for d in range(2):
                    ag_arrival(kind, s, d, p).wait_recv()
                    if send:
                        ag_copy(kind, s, d, p).start()
        for kind in kinds:
            for d in range(2):
                sa_copy(kind, s, d).start()

    def ag_b(s, send=True):
        for kind in kinds:
            for d in range(2):
                ag_arrival(kind, s, d, 2).wait_recv()
                if send:
                    ag_copy(kind, s, d, 2).start()
                fx_copy(kind, s, d).start()
        for kind in kinds:
            for d in range(2):
                sb_copy(kind, s, d).start()

    for kind in kinds:
        rs_step(kind, 7, last=True)
        for p in range(2):
            for d in range(2):
                a_copy(kind, d, p).start()
        for d in range(2):
            f[kind][out_unit(kind, 0, d, 3 * xh)] = g[kind][unit(kind, y, d, 3 * xh)]
            ag_copy(kind, 0, d, 2).start()
            fx_copy(kind, 0, d).start()
            sb_copy(kind, 0, d).start()
    gain_finish(1)
    z_step(1, 4)
    ag_b(1)
    for kind in kinds:
        for p in range(2):
            for d in range(2):
                a_copy(kind, d, p).wait_recv()
                f[kind][out_unit(kind, 0, d, mine_u[p])] = (
                    g[kind][unit(kind, y, d, mine_u[p])].astype(F32) + xa[kind, d, p].astype(F32)
                ).astype(BF16)
                ag_copy(kind, 0, d, p).start()
        for d in range(2):
            sa_copy(kind, 0, d).start()
    ag_b(2)

    @pl.loop(1, NY)
    def _(s):
        @pl.when(s < 7)
        def _():
            ag_a(s)

        @pl.when(s == 7)
        def _():
            ag_a(7, False)

        @pl.when(s < 5)
        def _():
            ag_b(s + 2)

        @pl.when(s == 5)
        def _():
            ag_b(7, False)

        x_arrived(s - 1)

        @pl.when(s < 3)
        def _():
            z_step(1, s + 4)

        @pl.when(s == 3)
        def _():
            z_step(1, 7, last=True)
            zx_copy(1).start()

        @pl.when(s == 2)
        def _():
            gain_finish(2)

        @pl.when(s == 4)
        def _():
            gain_finish(3)

        @pl.when(s == 6)
        def _():
            gain_finish(4)

    x_arrived(7)

    rows = pl.ds(pl.multiple_of(mp * OWN, OWN), OWN)
    own_tok = tok[rows, :].astype(F32)
    zx_copy(0).wait_recv()
    mixed[...] = (own_tok + (brp[xl, z].astype(F32) + zx[0].astype(F32))).astype(BF16)
    zx_copy(1).wait_recv()
    back_normed = bnp[xl, z].astype(F32) + zx[1].astype(F32)
    hat = (own_tok - mean[rows, :]) * inv[rows, :]
    back_hat = back_normed * gain[...]
    back_in = inv[rows, :] * (
        back_hat
        - jnp.mean(back_hat, axis=1, keepdims=True)
        - hat * jnp.mean(back_hat * hat, axis=1, keepdims=True)
    )
    gtok[...] = (cot[rows, :].astype(F32) + back_in).astype(BF16)
    gain_finish(5)
    ggain[...] = gacc[GAIN_ROUNDS]

    remote(fu, fu, s_sib, sib_r.at[0], sib).wait_recv()

    def all_sent(sem, ref):
        remote(ref, ref, sem, sib_r.at[0], sib).wait_send()

    all_sent(s_cot, cot.at[pl.ds(0, ROWS - OWN)])
    all_sent(s_ex, gu)
    all_sent(s_rs, rr)
    all_sent(s_x1, xr)
    all_sent(s_xa, xa)
    all_sent(s_z, zrecv)
    all_sent(s_zx, zx)
    all_sent(s_ag, rr)
    all_sent(s_sib, fu)
    all_sent(s_fx, xr)
    all_sent(s_gz, gz.at[pl.ds(0, NZ - 1)])
    all_sent(s_gn, gacc.at[pl.ds(0, GAIN_ROUNDS)])


def shards(tokens, layer_norm_gain, w_up, w_down, cotangent):
    anywhere = pl.BlockSpec(memory_space=pl.ANY)
    vmem = pl.BlockSpec(memory_space=pltpu.VMEM)
    dma = pltpu.SemaphoreType.DMA
    shapes = [((OWN, D), BF16), ((OWN, D), BF16), ((D, FF), BF16), ((FF, D), BF16), ((1, D), F32)]
    mixed, grad_tokens, grad_up, grad_down, gain_grad = pl.pallas_call(
        kernel,
        out_shape=tuple(pltpu.VMEM(shape, dtype) for shape, dtype in shapes),
        in_specs=[anywhere, vmem, anywhere, anywhere, anywhere],
        out_specs=(vmem,) * 5,
        scratch_shapes=[
            pltpu.VMEM((ROWS, D), BF16),
            pltpu.VMEM((D, FF), BF16),
            pltpu.VMEM((FF, D), BF16),
            pltpu.VMEM((ROWS, D), BF16),
            pltpu.VMEM((ROWS, 1), F32),
            pltpu.VMEM((ROWS, 1), F32),
            pltpu.VMEM((HALF, 2 * ROWS), BF16),
            pltpu.VMEM((HALF, ROWS), BF16),
            pltpu.VMEM((ROWS, D), BF16),
            pltpu.VMEM((ROWS, HALF), BF16),
            pltpu.VMEM((ROWS, FF), BF16),
            pltpu.VMEM((ROWS, FF), F32),
            pltpu.VMEM((FF, 2 * ROWS), BF16),
            pltpu.VMEM((2 * ROWS, FF), BF16),
            pltpu.VMEM((2, NZ, OWN, D), BF16),
            pltpu.VMEM((2, NZ, OWN, D), BF16),
            pltpu.VMEM((2, NZ - 1, 2, 2, OWN, HALF), BF16),
            pltpu.VMEM((2, OWN, D), BF16),
            pltpu.VMEM((HALF, FF), BF16),
            pltpu.VMEM((FF, HALF), BF16),
            pltpu.VMEM((2, NY - 1, 2, 3, UR, UW), BF16),
            pltpu.VMEM((2, NY, 2, UR, UW), BF16),
            pltpu.VMEM((2, 2, 2, UR, UW), BF16),
            pltpu.VMEM((NZ, 1, D), F32),
            pltpu.VMEM((GAIN_ROUNDS + 1, 1, D), F32),
            pltpu.VMEM((GAIN_ROUNDS, 1, D), F32),
            dma((4,)), dma((12,)),
            dma((2, 5, 2)), dma((4,)),
            dma((2, NY - 1, 2, 3)), dma((2, NY, 2)), dma((2, 2, 2)),
            dma((2, NZ - 1, 2)), dma((2,)),
            dma((2, NY - 1, 2, 3)), dma((1,)), dma((2, NY, 2)),
            dma((1,)), dma((GAIN_ROUNDS,)),
        ],
        compiler_params=pltpu.CompilerParams(
            collective_id=0, has_side_effects=True, vmem_limit_bytes=46 * 2**20
        ),
        cost_estimate=pl.CostEstimate(
            flops=12 * ROWS * D * FF, bytes_accessed=22 * 2**20, transcendentals=2 * ROWS * FF
        ),
        name="mlp_block",
    )(tokens, layer_norm_gain.reshape(1, D), w_up, w_down, cotangent)
    return mixed, grad_tokens, grad_up, grad_down, gain_grad.reshape(D)


def solution(mesh):
    placed = (P("dp", None), P(), P(None, "mp"), P("mp", None), P(("dp", "mp"), None))
    return jax.shard_map(
        shards,
        mesh=mesh,
        in_specs=placed,
        out_specs=(P(("dp", "mp"), None), P(("dp", "mp"), None), P(None, "mp"), P("mp", None), P()),
        check_vma=False,
    )
```

```python
import math

import jax
import jax.numpy as jnp
from jax import lax
from jax.experimental import pallas as pl
from jax.experimental.pallas import tpu as pltpu
from jax.sharding import PartitionSpec as P

F32 = jnp.float32
BF16 = jnp.bfloat16
D = 3072
HALF = D // 2
FF = 768
ROWS = 256
NY = 8
NZ = 8
OWN = 16
UC, DC = 192, 96
UR, UW = 48, 384
U, DN = 0, 1
GAIN_ROUNDS = 6


def gelu_value(pre):
    return 0.5 * pre * (1.0 + lax.erf(pre * (1.0 / math.sqrt(2.0))))


def gelu_slope(pre):
    cumul = 0.5 * (1.0 + lax.erf(pre * (1.0 / math.sqrt(2.0))))
    density = jnp.exp(-0.5 * pre * pre) * (1.0 / math.sqrt(2.0 * math.pi))
    return cumul + pre * density


def dot_nn(a, b):
    return lax.dot_general(a, b, (((1,), (0,)), ((), ())), preferred_element_type=F32)


def dot_nt(a, b):
    return lax.dot_general(a, b, (((1,), (1,)), ((), ())), preferred_element_type=F32)


def flat(*at):
    place = (at[0] * NY + at[1]) * 2 + at[2]
    return place if len(at) == 3 else place * 3 + at[3]


def mod8(v):
    return lax.rem(v + 16, 8)


def flip(v, b):
    return v + b - 2 * b * lax.rem(v // b, 2)


def kernel(
    tok_hbm, gain, wu_hbm, wd_hbm, cot_hbm,
    mixed, gtok, fu, fd, ggain,
    tok, wu, wd, nrm, mean, inv, nT, nTs, cot, cot_sib, act, slope, aT, bp, brp, bnp,
    zrecv, zx, gu, gd, rr, xr, xa, gz, gacc, grecv,
    lsem, sent, crsem, exr, rs_r, xs_r, xa_r, z_r, zx_r, ag_r, sib_r, fx_r, gz_r, gn_r,
):
    dp = lax.axis_index("dp")
    mp = lax.axis_index("mp")
    c = lax.rem(dp, 2)
    y = lax.rem(dp // 2, NY)
    xh = dp // 16
    z = lax.rem(mp, NZ)
    xl = mp // NZ

    s_cot, s_ex, s_rs, s_x1, s_xa, s_z, s_zx, s_ag, s_sib, s_fx, s_gz, s_gn = (sent.at[i] for i in range(12))

    def at_y(v):
        return (xh * 16 + v * 2 + c, mp)

    def at_z(v):
        return (dp, xl * NZ + v)

    sib = (dp + 1 - 2 * c, mp)
    xpart = (xh * -16 + 16 + y * 2 + c, mp)
    lpart = (dp, (1 - xl) * NZ + z)
    ydev = [at_y(mod8(y + 1)), at_y(mod8(y - 1))]
    zdev = [at_z(mod8(z + 1)), at_z(mod8(z - 1))]
    sign = [1, -1]

    def remote(src, dst, ssem, rsem, to):
        return pltpu.make_async_remote_copy(
            src_ref=src, dst_ref=dst, send_sem=ssem, recv_sem=rsem,
            device_id=to, device_id_type=pl.DeviceIdType.MESH,
        )

    load_cot = pltpu.make_async_copy(cot_hbm, cot.at[pl.ds(mp * OWN, OWN)], lsem.at[0])
    load_tok = pltpu.make_async_copy(tok_hbm, tok, lsem.at[1])
    load_wu = pltpu.make_async_copy(wu_hbm, wu, lsem.at[2])
    load_wd = pltpu.make_async_copy(wd_hbm, wd, lsem.at[3])
    for one in (load_cot, load_tok, load_wu, load_wd):
        one.start()
    barrier = pltpu.get_barrier_semaphore()
    zall = [at_z(mod8(z + j)) for j in range(1, NZ)]
    greet = ydev + zall + [sib, xpart, lpart, at_y(flip(y, 2)), at_y(flip(y, 4))]
    for one in greet:
        pl.semaphore_signal(barrier, inc=1, device_id=one, device_id_type=pl.DeviceIdType.MESH)
    pl.semaphore_wait(barrier, len(greet))

    def cot_half(k, h):
        return (pl.ds(pl.multiple_of((xl * NZ + k) * OWN, OWN), OWN), pl.ds(h * HALF, HALF))

    def cot_ring(k, j, d, h):
        ref = cot.at[cot_half(k, h)]
        return remote(ref, ref, s_cot, crsem.at[(j - 1) * 4 + d * 2 + h], zdev[d])

    def cot_send(j, d, h):
        cot_ring(mod8(z - sign[d] * (j - 1)), j, d, h).start()

    def cot_next(j, h):
        for d in range(2):
            if j == 4 and d != h:
                continue
            k = mod8(z - sign[d] * j)
            cot_ring(k, j, d, h).wait_recv()
            if j < 3 or (j == 3 and d == h):
                cot_send(j + 1, d, h)
            ref = cot.at[cot_half(k, h)]
            remote(ref, ref, s_cot, crsem.at[14], lpart).start()

    load_cot.wait()
    for h in range(2):
        for d in range(2):
            cot_send(1, d, h)
    mine = cot.at[pl.ds(pl.multiple_of(mp * OWN, OWN), OWN)]
    remote(mine, mine, s_cot, crsem.at[14], lpart).start()

    load_tok.wait()

    def layer_norm(lo, hi):
        @pl.loop(lo // 32, hi // 32)
        def _(i):
            rows = pl.ds(pl.multiple_of(i * 32, 32), 32)
            v = tok[rows, :].astype(F32)
            mu = jnp.mean(v, axis=1, keepdims=True)
            cen = v - mu
            iv = lax.rsqrt(jnp.mean(cen * cen, axis=1, keepdims=True) + 1e-06)
            mean[rows, :] = mu
            inv[rows, :] = iv
            nrm[rows, :] = (cen * iv * gain[...]).astype(BF16)

    layer_norm(0, ROWS)
    cot_next(1, 0)
    cot_next(1, 1)

    load_wu.wait()

    def pre_tile(t):
        cols = pl.ds(t * 256, 256)
        pre = dot_nn(nrm[...], wu[:, cols])
        a = gelu_value(pre)
        act[:, cols] = a.astype(BF16)
        slope[:, cols] = gelu_slope(pre)
        aT[cols, pl.ds(0, ROWS)] = a.T.astype(BF16)

    mineK, theirsK = pl.ds(0, ROWS), pl.ds(ROWS, ROWS)
    act_x = remote(aT.at[:, mineK], aT.at[:, theirsK], s_ex, exr.at[0], sib)

    pre_tile(0)
    cot_next(2, 0)
    cot_next(2, 1)
    pre_tile(1)
    cot_next(3, 0)
    cot_next(3, 1)
    pre_tile(2)
    act_x.start()
    cot_next(4, 0)
    cot_next(4, 1)

    @pl.loop(0, HALF // 256)
    def _(j):
        rows = pl.ds(pl.multiple_of(j * 256, 256), 256)
        own = pl.ds(pl.multiple_of(c * HALF + j * 256, 256), 256)
        other = pl.ds(pl.multiple_of((1 - c) * HALF + j * 256, 256), 256)
        nT[rows, mineK] = nrm[:, own].astype(F32).T.astype(BF16)
        nTs[rows, :] = nrm[:, other].astype(F32).T.astype(BF16)

    nrm_x = remote(nTs, nT.at[:, theirsK], s_ex, exr.at[1], sib)
    nrm_x.start()

    load_wd.wait()

    @pl.loop(0, D // 512)
    def _(t):
        cols = pl.ds(pl.multiple_of(t * 512, 512), 512)
        brp[:, :, :, cols] = dot_nn(act[...], wd[:, cols]).astype(BF16).reshape(2, NZ, OWN, 512)

    eight = cot.at[pl.ds(0, NZ * OWN)]
    remote(eight, eight, s_cot, crsem.at[14], lpart).wait_recv()

    ownC = pl.ds(pl.multiple_of(c * HALF, HALF), HALF)
    otherC = pl.ds(pl.multiple_of((1 - c) * HALF, HALF), HALF)
    cot_x = remote(cot.at[:, otherC], cot_sib, s_ex, exr.at[2], sib)
    cot_x.start()

    zp = (brp, bnp)

    def z_cols(s, d):
        return (slice(None), mod8(z - sign[d] * (1 + s)), slice(None), pl.ds(d * HALF, HALF))

    def z_copy(kind, s, d):
        return remote(
            zp[kind].at[z_cols(s, d)], zrecv.at[kind, s, d], s_z, z_r.at[flat(kind, s, d)], zdev[d],
        )

    def z_step(kind, s, first=False, last=False):
        for d in range(2):
            if not first:
                z_copy(kind, s - 1, d).wait_recv()
                zp[kind][z_cols(s, d)] = (
                    zp[kind][z_cols(s, d)].astype(F32) + zrecv[kind, s - 1, d].astype(F32)
                ).astype(BF16)
            if not last:
                z_copy(kind, s, d).start()

    def zx_copy(kind):
        return remote(zp[kind].at[1 - xl, z], zx.at[kind], s_zx, zx_r.at[kind], lpart)

    z_step(0, 0, first=True)

    @pl.loop(0, FF // 256)
    def _(t):
        rows = pl.ds(pl.multiple_of(t * 256, 256), 256)
        back = dot_nt(cot[...], wd[rows, :])
        bp[mineK, rows] = (back * slope[:, rows]).astype(BF16)

    bp_x = remote(bp.at[mineK], bp.at[theirsK], s_ex, exr.at[3], sib)
    bp_x.start()

    def unit(kind, k, d, u, n=1, base=0):
        if kind == U:
            return (pl.ds(pl.multiple_of(base + k * UC + u * UR, 16), n * UR), pl.ds(d * UW, UW))
        return (pl.ds(pl.multiple_of(k * DC + d * UR, 16), UR), pl.ds(pl.multiple_of(base + u * UW, 128), n * UW))

    g = (gu, gd)
    f = (fu, fd)
    kinds = (DN, U)
    mine_u = (1, 2, 3 * xh)

    def rs_chunk(s, d):
        return mod8(y - sign[d] * (1 + s))

    def x_first(kind, s, d):
        return remote(
            g[kind].at[unit(kind, rs_chunk(s, d), d, 3 - 3 * xh)], xr.at[kind, s, d],
            s_x1, xs_r.at[flat(kind, s, d)], xpart,
        )

    def x_first_start(kind, s):
        for d in range(2):
            x_first(kind, s, d).start()

    def rs_copy(kind, s, d, p):
        return remote(
            g[kind].at[unit(kind, rs_chunk(s, d), d, mine_u[p])], rr.at[kind, s, d, p],
            s_rs, rs_r.at[flat(kind, s, d, p)], ydev[d],
        )

    def rs_step(kind, s, pieces=(0, 1, 2), first=False, last=False):
        for p in pieces:
            for d in range(2):
                at = unit(kind, rs_chunk(s, d), d, mine_u[p])
                if p == 2:
                    x_first(kind, s, d).wait_recv()
                if not first:
                    rs_copy(kind, s - 1, d, p).wait_recv()
                if p == 2 or not first:
                    total = g[kind][at].astype(F32)
                    if p == 2:
                        total = total + xr[kind, s, d].astype(F32)
                    if not first:
                        total = total + rr[kind, s - 1, d, p].astype(F32)
                    g[kind][at] = total.astype(BF16)
                if not last:
                    rs_copy(kind, s, d, p).start()

    remote(aT.at[:, mineK], aT.at[:, theirsK], s_ex, exr.at[0], sib).wait_recv()
    remote(cot.at[:, otherC], cot_sib, s_ex, exr.at[2], sib).wait_recv()

    @pl.loop(0, HALF // 512)
    def _(t):
        cols = pl.ds(pl.multiple_of(t * 512, 512), 512)
        part = pl.ds(pl.multiple_of(c * HALF + t * 512, 512), 512)
        gd[:, cols] = (
            dot_nn(aT[:, mineK], cot[:, part]) + dot_nn(aT[:, theirsK], cot_sib[:, cols])
        ).astype(BF16)

    x_first_start(DN, 0)
    rs_step(DN, 0, (0, 1), first=True)
    x_first_start(DN, 1)

    remote(nTs, nT.at[:, theirsK], s_ex, exr.at[1], sib).wait_recv()
    remote(bp.at[mineK], bp.at[theirsK], s_ex, exr.at[3], sib).wait_recv()

    @pl.loop(0, HALF // 512)
    def _(t):
        rows = pl.ds(pl.multiple_of(t * 512, 512), 512)
        gu[rows, :] = dot_nn(nT[rows, :], bp[...]).astype(BF16)

    x_first_start(U, 0)
    rs_step(U, 0, (0, 1), first=True)
    x_first_start(U, 1)
    z_step(0, 1)


    partners = [at_y(flip(y, 1)), at_y(flip(y, 2)), at_y(flip(y, 4)), lpart, xpart, sib]

    def gz_copy(j):
        return remote(gz.at[z], gz.at[z], s_gz, gz_r.at[0], zall[j - 1])

    def gain_copy(r):
        return remote(gacc.at[r], grecv.at[r], s_gn, gn_r.at[r], partners[r])

    def gain_z_finish():
        seven = gz.at[pl.ds(0, NZ - 1)]
        remote(seven, seven, s_gz, gz_r.at[0], sib).wait_recv()
        total = gz[0]
        for k in range(1, NZ):
            total = total + gz[k]
        gacc[0] = total
        gain_copy(0).start()

    def gain_finish(r):
        gain_copy(r).wait_recv()
        gacc[r + 1] = gacc[r] + grecv[r]
        if r + 1 < GAIN_ROUNDS:
            gain_copy(r + 1).start()

    rs_step(DN, 0, (2,), first=True)
    x_first_start(DN, 2)

    @pl.loop(0, D // 512)
    def _(t):
        cols = pl.ds(pl.multiple_of(t * 512, 512), 512)
        back = dot_nt(bp[mineK, :], wu[cols, :])
        bnp[:, :, :, cols] = back.astype(BF16).reshape(2, NZ, OWN, 512)
        hat = (tok[:, cols].astype(F32) - mean[...]) * inv[...]
        gz[z, :, cols] = jnp.sum(back * hat, axis=0, keepdims=True)

    rs_step(U, 0, (2,), first=True)
    x_first_start(U, 2)
    z_step(0, 2)
    for j in range(1, NZ):
        gz_copy(j).start()

    @pl.loop(1, 7)
    def _(s):
        for kind in kinds:
            rs_step(kind, s)

            @pl.when(s < 6)
            def _():
                x_first_start(kind, s + 2)

        @pl.when(s < 5)
        def _():
            z_step(0, s + 2)

        @pl.when(s == 5)
        def _():
            z_step(0, 7, last=True)
            zx_copy(0).start()

        @pl.when(s == 3)
        def _():
            z_step(1, 0, first=True)

        @pl.when(s > 3)
        def _():
            z_step(1, s - 3)

        @pl.when(s == 3)
        def _():
            gain_z_finish()

        @pl.when(s == 5)
        def _():
            gain_finish(0)

    def a_copy(kind, d, p):
        return remote(
            g[kind].at[unit(kind, y, d, mine_u[p])], xa.at[kind, d, p], s_xa, xa_r.at[kind * 4 + d * 2 + p], xpart,
        )

    def ag_chunk(s, d):
        return mod8(y - sign[d] * s)

    def out_unit(kind, s, d, u, n=1):
        return unit(kind, ag_chunk(s, d), d, u, n, c * HALF)

    def own(kind, d, p):
        return xa.at[kind, d, p] if p < 2 else g[kind].at[unit(kind, y, d, 3 * xh)]

    def out_copy(kind, s, d, p, ssem, rsem, to):
        dst = f[kind].at[out_unit(kind, s, d, mine_u[p])]
        return remote(own(kind, d, p) if isinstance(s, int) and s == 0 else dst, dst, ssem, rsem, to)

    def ag_copy(kind, s, d, p):
        return out_copy(kind, s, d, p, s_ag, ag_r.at[flat(kind, s, d, p)], ydev[d])

    def ag_arrival(kind, s, d, p):
        at = f[kind].at[out_unit(kind, s, d, mine_u[p])]
        return remote(at, at, s_ag, ag_r.at[flat(kind, s - 1, d, p)], ydev[d])

    def sib_copy(kind, s, d, p):
        return out_copy(kind, s, d, p, s_sib, sib_r.at[0], sib)

    def sa_copy(kind, s, d):
        at = f[kind].at[out_unit(kind, s, d, 1, 2)]
        return remote(at, at, s_sib, sib_r.at[0], sib)

    def fx_copy(kind, s, d):
        return out_copy(kind, s, d, 2, s_fx, fx_r.at[flat(kind, s, d)], xpart)

    def keep(kind, d, p):
        return pltpu.make_async_copy(own(kind, d, p), f[kind].at[out_unit(kind, 0, d, mine_u[p])], lsem.at[4])

    def fx_arrival(kind, s, d):
        at = f[kind].at[out_unit(kind, s, d, 3 - 3 * xh)]
        return remote(at, at, s_fx, fx_r.at[flat(kind, s, d)], xpart)

    def sx_copy(kind, s, d):
        at = f[kind].at[out_unit(kind, s, d, 3 - 3 * xh)]
        return remote(at, at, s_sib, sib_r.at[0], sib)

    def x_arrived(s):
        for kind in kinds:
            for d in range(2):
                fx_arrival(kind, s, d).wait_recv()
                sx_copy(kind, s, d).start()

    def ag_a(s, send=True):
        for kind in kinds:
            for p in range(2):
                for d in range(2):
                    ag_arrival(kind, s, d, p).wait_recv()
                    if send:
                        ag_copy(kind, s, d, p).start()
        for kind in kinds:
            for d in range(2):
                sa_copy(kind, s, d).start()

    def ag_b(s, send=True):
        for kind in kinds:
            for d in range(2):
                ag_arrival(kind, s, d, 2).wait_recv()
                if send:
                    ag_copy(kind, s, d, 2).start()
                fx_copy(kind, s, d).start()
        for kind in kinds:
            for d in range(2):
                sib_copy(kind, s, d, 2).start()

    for kind in kinds:
        rs_step(kind, 7, last=True)
        for p in range(2):
            for d in range(2):
                a_copy(kind, d, p).start()
        for d in range(2):
            ag_copy(kind, 0, d, 2).start()
            fx_copy(kind, 0, d).start()
            sib_copy(kind, 0, d, 2).start()
            keep(kind, d, 2).start()
    gain_finish(1)
    z_step(1, 4)
    ag_b(1)
    for kind in kinds:
        for p in range(2):
            for d in range(2):
                a_copy(kind, d, p).wait_recv()
                at = unit(kind, y, d, mine_u[p])
                xa[kind, d, p] = (g[kind][at].astype(F32) + xa[kind, d, p].astype(F32)).astype(BF16)
                ag_copy(kind, 0, d, p).start()
                sib_copy(kind, 0, d, p).start()
                keep(kind, d, p).start()
    ag_b(2)

    @pl.loop(1, NY)
    def _(s):
        @pl.when(s < 7)
        def _():
            ag_a(s)

        @pl.when(s == 7)
        def _():
            ag_a(7, False)

        @pl.when(s < 5)
        def _():
            ag_b(s + 2)

        @pl.when(s == 5)
        def _():
            ag_b(7, False)

        x_arrived(s - 1)

        @pl.when(s < 3)
        def _():
            z_step(1, s + 4)

        @pl.when(s == 3)
        def _():
            z_step(1, 7, last=True)
            zx_copy(1).start()

        @pl.when(s == 2)
        def _():
            gain_finish(2)

        @pl.when(s == 4)
        def _():
            gain_finish(3)

        @pl.when(s == 6)
        def _():
            gain_finish(4)

    x_arrived(7)

    rows = pl.ds(pl.multiple_of(mp * OWN, OWN), OWN)
    own_tok = tok[rows, :].astype(F32)
    zx_copy(0).wait_recv()
    mixed[...] = (own_tok + (brp[xl, z].astype(F32) + zx[0].astype(F32))).astype(BF16)
    zx_copy(1).wait_recv()
    back_normed = bnp[xl, z].astype(F32) + zx[1].astype(F32)
    hat = (own_tok - mean[rows, :]) * inv[rows, :]
    back_hat = back_normed * gain[...]
    back_in = inv[rows, :] * (
        back_hat
        - jnp.mean(back_hat, axis=1, keepdims=True)
        - hat * jnp.mean(back_hat * hat, axis=1, keepdims=True)
    )
    gtok[...] = (cot[rows, :].astype(F32) + back_in).astype(BF16)
    gain_finish(5)
    ggain[...] = gacc[GAIN_ROUNDS]

    remote(fu, fu, s_sib, sib_r.at[0], sib).wait_recv()

    def all_sent(sem, ref):
        remote(ref, ref, sem, sib_r.at[0], sib).wait_send()

    pltpu.make_async_copy(rr.at[0, pl.ds(0, 2)], rr.at[1, pl.ds(0, 2)], lsem.at[4]).wait()
    all_sent(s_cot, cot.at[pl.ds(0, ROWS - OWN)])
    all_sent(s_ex, gu)
    all_sent(s_rs, rr)
    all_sent(s_x1, xr)
    all_sent(s_xa, xa)
    all_sent(s_z, zrecv)
    all_sent(s_zx, zx)
    all_sent(s_ag, rr)
    all_sent(s_sib, fu)
    all_sent(s_fx, xr)
    all_sent(s_gz, gz.at[pl.ds(0, NZ - 1)])
    all_sent(s_gn, gacc.at[pl.ds(0, GAIN_ROUNDS)])


def store(*refs):
    sem = refs[-1]
    copies = []
    for i in range(5):
        rows = refs[i].shape[0]
        parts = 4 if rows > OWN else 1
        for j in range(parts):
            at = pl.ds(j * (rows // parts), rows // parts)
            copies.append(pltpu.make_async_copy(refs[i].at[at], refs[5 + i].at[at], sem.at[len(copies)]))
    for one in copies:
        one.start()
    for one in copies:
        one.wait()


def shards(tokens, layer_norm_gain, w_up, w_down, cotangent):
    anywhere = pl.BlockSpec(memory_space=pl.ANY)
    vmem = pl.BlockSpec(memory_space=pltpu.VMEM)
    dma = pltpu.SemaphoreType.DMA
    shapes = [((OWN, D), BF16), ((OWN, D), BF16), ((D, FF), BF16), ((FF, D), BF16), ((1, D), F32)]
    held = pl.pallas_call(
        kernel,
        out_shape=tuple(pltpu.VMEM(shape, dtype) for shape, dtype in shapes),
        in_specs=[anywhere, vmem, anywhere, anywhere, anywhere],
        out_specs=(vmem, vmem, anywhere, anywhere, vmem),
        scratch_shapes=[
            pltpu.VMEM((ROWS, D), BF16),
            pltpu.VMEM((D, FF), BF16),
            pltpu.VMEM((FF, D), BF16),
            pltpu.VMEM((ROWS, D), BF16),
            pltpu.VMEM((ROWS, 1), F32),
            pltpu.VMEM((ROWS, 1), F32),
            pltpu.VMEM((HALF, 2 * ROWS), BF16),
            pltpu.VMEM((HALF, ROWS), BF16),
            pltpu.VMEM((ROWS, D), BF16),
            pltpu.VMEM((ROWS, HALF), BF16),
            pltpu.VMEM((ROWS, FF), BF16),
            pltpu.VMEM((ROWS, FF), F32),
            pltpu.VMEM((FF, 2 * ROWS), BF16),
            pltpu.VMEM((2 * ROWS, FF), BF16),
            pltpu.VMEM((2, NZ, OWN, D), BF16),
            pltpu.VMEM((2, NZ, OWN, D), BF16),
            pltpu.VMEM((2, NZ - 1, 2, 2, OWN, HALF), BF16),
            pltpu.VMEM((2, OWN, D), BF16),
            pltpu.VMEM((HALF, FF), BF16),
            pltpu.VMEM((FF, HALF), BF16),
            pltpu.VMEM((2, NY - 1, 2, 3, UR, UW), BF16),
            pltpu.VMEM((2, NY, 2, UR, UW), BF16),
            pltpu.VMEM((2, 2, 2, UR, UW), BF16),
            pltpu.VMEM((NZ, 1, D), F32),
            pltpu.VMEM((GAIN_ROUNDS + 1, 1, D), F32),
            pltpu.VMEM((GAIN_ROUNDS, 1, D), F32),
            dma((5,)), dma((12,)),
            dma((16,)), dma((4,)),
            dma((90,)), dma((32,)), dma((8,)),
            dma((30,)), dma((2,)),
            dma((90,)), dma((1,)), dma((32,)),
            dma((1,)), dma((GAIN_ROUNDS,)),
        ],
        compiler_params=pltpu.CompilerParams(
            collective_id=0, has_side_effects=True, vmem_limit_bytes=46 * 2**20
        ),
        cost_estimate=pl.CostEstimate(
            flops=12 * ROWS * D * FF, bytes_accessed=22 * 2**20, transcendentals=2 * ROWS * FF
        ),
        name="mlp_block",
    )(tokens, layer_norm_gain.reshape(1, D), w_up, w_down, cotangent)
    mixed, grad_tokens, grad_up, grad_down, gain_grad = pl.pallas_call(
        store,
        out_shape=tuple(jax.ShapeDtypeStruct(shape, dtype) for shape, dtype in shapes),
        in_specs=[vmem] * 5,
        out_specs=(anywhere,) * 5,
        scratch_shapes=[dma((11,))],
        compiler_params=pltpu.CompilerParams(vmem_limit_bytes=2**20),
        cost_estimate=pl.CostEstimate(flops=0, bytes_accessed=10 * 2**20, transcendentals=0),
        name="store",
    )(*(pltpu.with_memory_space_constraint(one, pltpu.VMEM) for one in held))
    return mixed, grad_tokens, grad_up, grad_down, gain_grad.reshape(D)


def solution(mesh):
    placed = (P("dp", None), P(), P(None, "mp"), P("mp", None), P(("dp", "mp"), None))
    return jax.shard_map(
        shards,
        mesh=mesh,
        in_specs=placed,
        out_specs=(P(("dp", "mp"), None), P(("dp", "mp"), None), P(None, "mp"), P("mp", None), P()),
        check_vma=False,
    )
```

```python
import math

import jax
import jax.numpy as jnp
from jax import lax
from jax.experimental import pallas as pl
from jax.experimental.pallas import tpu as pltpu
from jax.sharding import PartitionSpec as P

F32 = jnp.float32
BF16 = jnp.bfloat16
D = 3072
HALF = D // 2
FF = 768
ROWS = 256
NY = 8
NZ = 8
OWN = 16
UC, DC = 192, 96
UR, DR, UW = 64, 48, 384
U, DN = 0, 1
GAIN_ROUNDS = 6


def gelu_value(pre):
    return 0.5 * pre * (1.0 + lax.erf(pre * (1.0 / math.sqrt(2.0))))


def gelu_slope(pre):
    cumul = 0.5 * (1.0 + lax.erf(pre * (1.0 / math.sqrt(2.0))))
    density = jnp.exp(-0.5 * pre * pre) * (1.0 / math.sqrt(2.0 * math.pi))
    return cumul + pre * density


def dot_nn(a, b):
    return lax.dot_general(a, b, (((1,), (0,)), ((), ())), preferred_element_type=F32)


def dot_nt(a, b):
    return lax.dot_general(a, b, (((1,), (1,)), ((), ())), preferred_element_type=F32)


def flat(*at):
    place = (at[0] * NY + at[1]) * 2 + at[2]
    return place if len(at) == 3 else place * 2 + at[3]


def mod8(v):
    return lax.rem(v + 16, 8)


def flip(v, b):
    return v + b - 2 * b * lax.rem(v // b, 2)


def kernel(
    tok_hbm, gain, wu_hbm, wd_hbm, cot_hbm,
    mixed, gtok, fu, fd, ggain,
    tok, wu, wd, nrm, mean, inv, nT, nTs, cot, cot_sib, act, slope, aT, bp, brp, bnp,
    zrecv, zx, gu, gd, rau, rad, rbu, rbd, xru, xrd, xau, xad, gz, gacc, grecv,
    lsem, sent, crsem, exr, rs_r, xs_r, xa_r, z_r, zx_r, ag_r, sib_r, fx_r, gz_r, gn_r,
):
    dp = lax.axis_index("dp")
    mp = lax.axis_index("mp")
    c = lax.rem(dp, 2)
    y = lax.rem(dp // 2, NY)
    xh = dp // 16
    z = lax.rem(mp, NZ)
    xl = mp // NZ

    s_cot, s_ex, s_z, s_zx, s_sib, s_gz, s_gn = (sent.at[i] for i in range(7))
    s_rs, s_ag = (tuple(sent.at[7 + 4 * j + i] for i in range(4)) for j in range(2))
    s_x1, s_xa, s_fx = (tuple(sent.at[15 + 2 * j + i] for i in range(2)) for j in range(3))

    def at_y(v):
        return (xh * 16 + v * 2 + c, mp)

    def at_z(v):
        return (dp, xl * NZ + v)

    sib = (dp + 1 - 2 * c, mp)
    xpart = (xh * -16 + 16 + y * 2 + c, mp)
    lpart = (dp, (1 - xl) * NZ + z)
    ydev = [at_y(mod8(y + 1)), at_y(mod8(y - 1))]
    zdev = [at_z(mod8(z + 1)), at_z(mod8(z - 1))]
    sign = [1, -1]

    def remote(src, dst, ssem, rsem, to):
        return pltpu.make_async_remote_copy(
            src_ref=src, dst_ref=dst, send_sem=ssem, recv_sem=rsem,
            device_id=to, device_id_type=pl.DeviceIdType.MESH,
        )

    load_cot = pltpu.make_async_copy(cot_hbm, cot.at[pl.ds(mp * OWN, OWN)], lsem.at[0])
    load_tok = pltpu.make_async_copy(tok_hbm, tok, lsem.at[1])
    load_wu = pltpu.make_async_copy(wu_hbm, wu, lsem.at[2])
    load_wd = pltpu.make_async_copy(wd_hbm, wd, lsem.at[3])
    for one in (load_cot, load_tok, load_wu, load_wd):
        one.start()
    barrier = pltpu.get_barrier_semaphore()
    zall = [at_z(mod8(z + j)) for j in range(1, NZ)]
    greet = ydev + zall + [sib, xpart, lpart, at_y(flip(y, 2)), at_y(flip(y, 4))]
    for one in greet:
        pl.semaphore_signal(barrier, inc=1, device_id=one, device_id_type=pl.DeviceIdType.MESH)
    pl.semaphore_wait(barrier, len(greet))

    def cot_half(k, h):
        return (pl.ds(pl.multiple_of((xl * NZ + k) * OWN, OWN), OWN), pl.ds(h * HALF, HALF))

    def cot_ring(k, j, d, h):
        ref = cot.at[cot_half(k, h)]
        return remote(ref, ref, s_cot, crsem.at[(j - 1) * 4 + d * 2 + h], zdev[d])

    def cot_send(j, d, h):
        cot_ring(mod8(z - sign[d] * (j - 1)), j, d, h).start()

    def cot_next(j, h):
        for d in range(2):
            if j == 4 and d != h:
                continue
            k = mod8(z - sign[d] * j)
            cot_ring(k, j, d, h).wait_recv()
            if j < 3 or (j == 3 and d == h):
                cot_send(j + 1, d, h)
            ref = cot.at[cot_half(k, h)]
            remote(ref, ref, s_cot, crsem.at[14], lpart).start()

    load_cot.wait()
    for h in range(2):
        for d in range(2):
            cot_send(1, d, h)
    mine = cot.at[pl.ds(pl.multiple_of(mp * OWN, OWN), OWN)]
    remote(mine, mine, s_cot, crsem.at[14], lpart).start()

    load_tok.wait()

    def layer_norm(lo, hi):
        @pl.loop(lo // 32, hi // 32)
        def _(i):
            rows = pl.ds(pl.multiple_of(i * 32, 32), 32)
            v = tok[rows, :].astype(F32)
            mu = jnp.mean(v, axis=1, keepdims=True)
            cen = v - mu
            iv = lax.rsqrt(jnp.mean(cen * cen, axis=1, keepdims=True) + 1e-06)
            mean[rows, :] = mu
            inv[rows, :] = iv
            nrm[rows, :] = (cen * iv * gain[...]).astype(BF16)

    layer_norm(0, ROWS)
    cot_next(1, 0)
    cot_next(1, 1)

    load_wu.wait()

    def pre_tile(t):
        cols = pl.ds(t * 256, 256)
        pre = dot_nn(nrm[...], wu[:, cols])
        a = gelu_value(pre)
        act[:, cols] = a.astype(BF16)
        slope[:, cols] = gelu_slope(pre)
        aT[cols, pl.ds(0, ROWS)] = a.T.astype(BF16)

    mineK, theirsK = pl.ds(0, ROWS), pl.ds(ROWS, ROWS)
    act_x = remote(aT.at[:, mineK], aT.at[:, theirsK], s_ex, exr.at[0], sib)

    pre_tile(0)
    cot_next(2, 0)
    cot_next(2, 1)
    pre_tile(1)
    cot_next(3, 0)
    cot_next(3, 1)
    pre_tile(2)
    act_x.start()
    cot_next(4, 0)
    cot_next(4, 1)

    @pl.loop(0, HALF // 256)
    def _(j):
        rows = pl.ds(pl.multiple_of(j * 256, 256), 256)
        own = pl.ds(pl.multiple_of(c * HALF + j * 256, 256), 256)
        other = pl.ds(pl.multiple_of((1 - c) * HALF + j * 256, 256), 256)
        nT[rows, mineK] = nrm[:, own].astype(F32).T.astype(BF16)
        nTs[rows, :] = nrm[:, other].astype(F32).T.astype(BF16)

    nrm_x = remote(nTs, nT.at[:, theirsK], s_ex, exr.at[1], sib)
    nrm_x.start()

    load_wd.wait()

    @pl.loop(0, D // 512)
    def _(t):
        cols = pl.ds(pl.multiple_of(t * 512, 512), 512)
        brp[:, :, :, cols] = dot_nn(act[...], wd[:, cols]).astype(BF16).reshape(2, NZ, OWN, 512)

    eight = cot.at[pl.ds(0, NZ * OWN)]
    remote(eight, eight, s_cot, crsem.at[14], lpart).wait_recv()

    ownC = pl.ds(pl.multiple_of(c * HALF, HALF), HALF)
    otherC = pl.ds(pl.multiple_of((1 - c) * HALF, HALF), HALF)
    cot_x = remote(cot.at[:, otherC], cot_sib, s_ex, exr.at[2], sib)
    cot_x.start()

    zp = (brp, bnp)

    def z_cols(s, d):
        return (slice(None), mod8(z - sign[d] * (1 + s)), slice(None), pl.ds(d * HALF, HALF))

    def z_copy(kind, s, d):
        return remote(
            zp[kind].at[z_cols(s, d)], zrecv.at[kind, s, d], s_z, z_r.at[flat(kind, s, d)], zdev[d],
        )

    def z_step(kind, s, first=False, last=False):
        for d in range(2):
            if not first:
                z_copy(kind, s - 1, d).wait_recv()
                zp[kind][z_cols(s, d)] = (
                    zp[kind][z_cols(s, d)].astype(F32) + zrecv[kind, s - 1, d].astype(F32)
                ).astype(BF16)
            if not last:
                z_copy(kind, s, d).start()

    def zx_copy(kind):
        return remote(zp[kind].at[1 - xl, z], zx.at[kind], s_zx, zx_r.at[kind], lpart)

    z_step(0, 0, first=True)

    @pl.loop(0, FF // 256)
    def _(t):
        rows = pl.ds(pl.multiple_of(t * 256, 256), 256)
        back = dot_nt(cot[...], wd[rows, :])
        bp[mineK, rows] = (back * slope[:, rows]).astype(BF16)

    bp_x = remote(bp.at[mineK], bp.at[theirsK], s_ex, exr.at[3], sib)
    bp_x.start()

    def unit(kind, k, d, u, n=1, base=0):
        if kind == U:
            return (pl.ds(pl.multiple_of(base + k * UC + u * UR, 16), n * UR), pl.ds(d * UW, UW))
        return (pl.ds(pl.multiple_of(k * DC + d * DR, 16), DR), pl.ds(pl.multiple_of(base + u * UW, 128), n * UW))

    g = (gu, gd)
    f = (fu, fd)
    kinds = (DN, U)
    top = (2, 3)
    ra, rb, xr, xa = (rau, rad), (rbu, rbd), (xru, xrd), (xau, xad)

    def piece(kind, p):
        return (1, top[kind] - 1) if p == 0 else (top[kind] * xh, 1)

    def other(kind):
        return top[kind] * (1 - xh)

    def sort(kind, p):
        return kind + 2 * p

    def rs_chunk(s, d):
        return mod8(y - sign[d] * (1 + s))

    def x_first(kind, s, d):
        return remote(
            g[kind].at[unit(kind, rs_chunk(s, d), d, other(kind))], xr[kind].at[s, d],
            s_x1[kind], xs_r.at[flat(kind, s, d)], xpart,
        )

    def x_first_start(kind, s):
        for d in range(2):
            x_first(kind, s, d).start()

    def rs_slot(kind, s, d, p):
        return (ra, rb)[p][kind].at[s, d]

    def rs_copy(kind, s, d, p):
        return remote(
            g[kind].at[unit(kind, rs_chunk(s, d), d, *piece(kind, p))], rs_slot(kind, s, d, p),
            s_rs[sort(kind, p)], rs_r.at[flat(kind, s, d, p)], ydev[d],
        )

    def rs_step(kind, s, which=(0, 1), first=False, last=False):
        for p in which:
            for d in range(2):
                at = unit(kind, rs_chunk(s, d), d, *piece(kind, p))
                if p == 1:
                    x_first(kind, s, d).wait_recv()
                if not first:
                    rs_copy(kind, s - 1, d, p).wait_recv()
                if p == 1 or not first:
                    total = g[kind][at].astype(F32)
                    if p == 1:
                        total = total + xr[kind][s, d].astype(F32)
                    if not first:
                        total = total + rs_slot(kind, s - 1, d, p)[...].astype(F32)
                    g[kind][at] = total.astype(BF16)
                if not last:
                    rs_copy(kind, s, d, p).start()

    remote(aT.at[:, mineK], aT.at[:, theirsK], s_ex, exr.at[0], sib).wait_recv()
    remote(cot.at[:, otherC], cot_sib, s_ex, exr.at[2], sib).wait_recv()

    @pl.loop(0, HALF // 512)
    def _(t):
        cols = pl.ds(pl.multiple_of(t * 512, 512), 512)
        part = pl.ds(pl.multiple_of(c * HALF + t * 512, 512), 512)
        gd[:, cols] = (
            dot_nn(aT[:, mineK], cot[:, part]) + dot_nn(aT[:, theirsK], cot_sib[:, cols])
        ).astype(BF16)

    x_first_start(DN, 0)
    rs_step(DN, 0, (0,), first=True)
    x_first_start(DN, 1)

    remote(nTs, nT.at[:, theirsK], s_ex, exr.at[1], sib).wait_recv()
    remote(bp.at[mineK], bp.at[theirsK], s_ex, exr.at[3], sib).wait_recv()

    @pl.loop(0, HALF // 512)
    def _(t):
        rows = pl.ds(pl.multiple_of(t * 512, 512), 512)
        gu[rows, :] = dot_nn(nT[rows, :], bp[...]).astype(BF16)

    x_first_start(U, 0)
    rs_step(U, 0, (0,), first=True)
    x_first_start(U, 1)
    z_step(0, 1)


    partners = [at_y(flip(y, 1)), at_y(flip(y, 2)), at_y(flip(y, 4)), lpart, xpart, sib]

    def gz_copy(j):
        return remote(gz.at[z], gz.at[z], s_gz, gz_r.at[0], zall[j - 1])

    def gain_copy(r):
        return remote(gacc.at[r], grecv.at[r], s_gn, gn_r.at[r], partners[r])

    def gain_z_finish():
        seven = gz.at[pl.ds(0, NZ - 1)]
        remote(seven, seven, s_gz, gz_r.at[0], sib).wait_recv()
        total = gz[0]
        for k in range(1, NZ):
            total = total + gz[k]
        gacc[0] = total
        gain_copy(0).start()

    def gain_finish(r):
        gain_copy(r).wait_recv()
        gacc[r + 1] = gacc[r] + grecv[r]
        if r + 1 < GAIN_ROUNDS:
            gain_copy(r + 1).start()

    rs_step(DN, 0, (1,), first=True)
    x_first_start(DN, 2)

    @pl.loop(0, D // 512)
    def _(t):
        cols = pl.ds(pl.multiple_of(t * 512, 512), 512)
        back = dot_nt(bp[mineK, :], wu[cols, :])
        bnp[:, :, :, cols] = back.astype(BF16).reshape(2, NZ, OWN, 512)
        hat = (tok[:, cols].astype(F32) - mean[...]) * inv[...]
        gz[z, :, cols] = jnp.sum(back * hat, axis=0, keepdims=True)

    rs_step(U, 0, (1,), first=True)
    x_first_start(U, 2)
    z_step(0, 2)
    for j in range(1, NZ):
        gz_copy(j).start()

    @pl.loop(1, 7)
    def _(s):
        for kind in kinds:
            rs_step(kind, s)

            @pl.when(s < 6)
            def _():
                x_first_start(kind, s + 2)

        @pl.when(s < 5)
        def _():
            z_step(0, s + 2)

        @pl.when(s == 5)
        def _():
            z_step(0, 7, last=True)
            zx_copy(0).start()

        @pl.when(s == 3)
        def _():
            z_step(1, 0, first=True)

        @pl.when(s > 3)
        def _():
            z_step(1, s - 3)

        @pl.when(s == 3)
        def _():
            gain_z_finish()

        @pl.when(s == 5)
        def _():
            gain_finish(0)

    def a_copy(kind, d):
        return remote(
            g[kind].at[unit(kind, y, d, *piece(kind, 0))], xa[kind].at[d], s_xa[kind], xa_r.at[kind * 2 + d], xpart,
        )

    def ag_chunk(s, d):
        return mod8(y - sign[d] * s)

    def out_unit(kind, s, d, u, n=1):
        return unit(kind, ag_chunk(s, d), d, u, n, c * HALF)

    def own(kind, d, p):
        return xa[kind].at[d] if p == 0 else g[kind].at[unit(kind, y, d, *piece(kind, 1))]

    def out_copy(kind, s, d, p, ssem, rsem, to):
        dst = f[kind].at[out_unit(kind, s, d, *piece(kind, p))]
        return remote(own(kind, d, p) if isinstance(s, int) and s == 0 else dst, dst, ssem, rsem, to)

    def ag_copy(kind, s, d, p):
        return out_copy(kind, s, d, p, s_ag[sort(kind, p)], ag_r.at[flat(kind, s, d, p)], ydev[d])

    def ag_arrival(kind, s, d, p):
        at = f[kind].at[out_unit(kind, s, d, *piece(kind, p))]
        return remote(at, at, s_ag[sort(kind, p)], ag_r.at[flat(kind, s - 1, d, p)], ydev[d])

    def own_to_sib(kind, d, p):
        return out_copy(kind, 0, d, p, s_sib, sib_r.at[0], sib)

    def fx_copy(kind, s, d):
        return out_copy(kind, s, d, 1, s_fx[kind], fx_r.at[flat(kind, s, d)], xpart)

    def keep(kind, d, p):
        dst = f[kind].at[out_unit(kind, 0, d, *piece(kind, p))]
        return pltpu.make_async_copy(own(kind, d, p), dst, lsem.at[4 + sort(kind, p)])

    def fx_arrival(kind, s, d):
        at = f[kind].at[out_unit(kind, s, d, other(kind))]
        return remote(at, at, s_fx[kind], fx_r.at[flat(kind, s, d)], xpart)

    def to_sib(kind, s, d, u, n):
        at = f[kind].at[out_unit(kind, s, d, u, n)]
        return remote(at, at, s_sib, sib_r.at[0], sib)

    def x_arrived(s):
        for kind in kinds:
            for d in range(2):
                fx_arrival(kind, s, d).wait_recv()
                if isinstance(s, int) and s == 0:
                    to_sib(kind, s, d, other(kind), 1).start()
                else:
                    to_sib(kind, s, d, 0, top[kind] + 1).start()

    def ag_a(s, send=True):
        for kind in kinds:
            for d in range(2):
                ag_arrival(kind, s, d, 0).wait_recv()
                if send:
                    ag_copy(kind, s, d, 0).start()

    def ag_b(s, send=True):
        for kind in kinds:
            for d in range(2):
                ag_arrival(kind, s, d, 1).wait_recv()
                if send:
                    ag_copy(kind, s, d, 1).start()
                fx_copy(kind, s, d).start()

    for kind in kinds:
        rs_step(kind, 7, last=True)
        for d in range(2):
            a_copy(kind, d).start()
        for d in range(2):
            ag_copy(kind, 0, d, 1).start()
            fx_copy(kind, 0, d).start()
    for kind in kinds:
        for d in range(2):
            own_to_sib(kind, d, 1).start()
            keep(kind, d, 1).start()
    gain_finish(1)
    z_step(1, 4)
    ag_b(1)
    for kind in kinds:
        for d in range(2):
            a_copy(kind, d).wait_recv()
            xa[kind][d] = (g[kind][unit(kind, y, d, *piece(kind, 0))].astype(F32) + xa[kind][d].astype(F32)).astype(BF16)
            ag_copy(kind, 0, d, 0).start()
    ag_b(2)
    for kind in kinds:
        for d in range(2):
            own_to_sib(kind, d, 0).start()
            keep(kind, d, 0).start()
    x_arrived(0)

    @pl.loop(1, NY)
    def _(s):
        @pl.when(s < 7)
        def _():
            ag_a(s)

        @pl.when(s == 7)
        def _():
            ag_a(7, False)

        @pl.when(s < 5)
        def _():
            ag_b(s + 2)

        @pl.when(s == 5)
        def _():
            ag_b(7, False)

        @pl.when(s > 1)
        def _():
            x_arrived(s - 1)

        @pl.when(s < 3)
        def _():
            z_step(1, s + 4)

        @pl.when(s == 3)
        def _():
            z_step(1, 7, last=True)
            zx_copy(1).start()

        @pl.when(s == 2)
        def _():
            gain_finish(2)

        @pl.when(s == 4)
        def _():
            gain_finish(3)

        @pl.when(s == 6)
        def _():
            gain_finish(4)

    x_arrived(7)

    rows = pl.ds(pl.multiple_of(mp * OWN, OWN), OWN)
    own_tok = tok[rows, :].astype(F32)
    zx_copy(0).wait_recv()
    mixed[...] = (own_tok + (brp[xl, z].astype(F32) + zx[0].astype(F32))).astype(BF16)
    zx_copy(1).wait_recv()
    back_normed = bnp[xl, z].astype(F32) + zx[1].astype(F32)
    hat = (own_tok - mean[rows, :]) * inv[rows, :]
    back_hat = back_normed * gain[...]
    back_in = inv[rows, :] * (
        back_hat
        - jnp.mean(back_hat, axis=1, keepdims=True)
        - hat * jnp.mean(back_hat * hat, axis=1, keepdims=True)
    )
    gtok[...] = (cot[rows, :].astype(F32) + back_in).astype(BF16)
    gain_finish(5)
    ggain[...] = gacc[GAIN_ROUNDS]

    remote(fu, fu, s_sib, sib_r.at[0], sib).wait_recv()

    def all_sent(sem, ref):
        remote(ref, ref, sem, sib_r.at[0], sib).wait_send()

    for i, ref in enumerate((xau, xad, xru.at[0], xrd.at[0])):
        pltpu.make_async_copy(ref, ref, lsem.at[4 + i]).wait()
    all_sent(s_cot, cot.at[pl.ds(0, ROWS - OWN)])
    all_sent(s_ex, gu)
    for i, ref in enumerate((rau, rad, rbu, rbd)):
        all_sent(s_rs[i], ref)
        all_sent(s_ag[i], ref)
    for kind in kinds:
        all_sent(s_xa[kind], xa[kind])
        all_sent(s_x1[kind], xr[kind])
        all_sent(s_fx[kind], xr[kind])
    all_sent(s_z, zrecv)
    all_sent(s_zx, zx)
    all_sent(s_sib, fu)
    all_sent(s_gz, gz.at[pl.ds(0, NZ - 1)])
    all_sent(s_gn, gacc.at[pl.ds(0, GAIN_ROUNDS)])


def store(*refs):
    sem = refs[-1]
    copies = []
    for i in range(5):
        rows = refs[i].shape[0]
        parts = 4 if rows > OWN else 1
        for j in range(parts):
            at = pl.ds(j * (rows // parts), rows // parts)
            copies.append(pltpu.make_async_copy(refs[i].at[at], refs[5 + i].at[at], sem.at[len(copies)]))
    for one in copies:
        one.start()
    for one in copies:
        one.wait()


def shards(tokens, layer_norm_gain, w_up, w_down, cotangent):
    anywhere = pl.BlockSpec(memory_space=pl.ANY)
    vmem = pl.BlockSpec(memory_space=pltpu.VMEM)
    dma = pltpu.SemaphoreType.DMA
    shapes = [((OWN, D), BF16), ((OWN, D), BF16), ((D, FF), BF16), ((FF, D), BF16), ((1, D), F32)]
    held = pl.pallas_call(
        kernel,
        out_shape=tuple(pltpu.VMEM(shape, dtype) for shape, dtype in shapes),
        in_specs=[anywhere, vmem, anywhere, anywhere, anywhere],
        out_specs=(vmem, vmem, anywhere, anywhere, vmem),
        scratch_shapes=[
            pltpu.VMEM((ROWS, D), BF16),
            pltpu.VMEM((D, FF), BF16),
            pltpu.VMEM((FF, D), BF16),
            pltpu.VMEM((ROWS, D), BF16),
            pltpu.VMEM((ROWS, 1), F32),
            pltpu.VMEM((ROWS, 1), F32),
            pltpu.VMEM((HALF, 2 * ROWS), BF16),
            pltpu.VMEM((HALF, ROWS), BF16),
            pltpu.VMEM((ROWS, D), BF16),
            pltpu.VMEM((ROWS, HALF), BF16),
            pltpu.VMEM((ROWS, FF), BF16),
            pltpu.VMEM((ROWS, FF), F32),
            pltpu.VMEM((FF, 2 * ROWS), BF16),
            pltpu.VMEM((2 * ROWS, FF), BF16),
            pltpu.VMEM((2, NZ, OWN, D), BF16),
            pltpu.VMEM((2, NZ, OWN, D), BF16),
            pltpu.VMEM((2, NZ - 1, 2, 2, OWN, HALF), BF16),
            pltpu.VMEM((2, OWN, D), BF16),
            pltpu.VMEM((HALF, FF), BF16),
            pltpu.VMEM((FF, HALF), BF16),
            pltpu.VMEM((NY - 1, 2, UR, UW), BF16),
            pltpu.VMEM((NY - 1, 2, DR, 2 * UW), BF16),
            pltpu.VMEM((NY - 1, 2, UR, UW), BF16),
            pltpu.VMEM((NY - 1, 2, DR, UW), BF16),
            pltpu.VMEM((NY, 2, UR, UW), BF16),
            pltpu.VMEM((NY, 2, DR, UW), BF16),
            pltpu.VMEM((2, UR, UW), BF16),
            pltpu.VMEM((2, DR, 2 * UW), BF16),
            pltpu.VMEM((NZ, 1, D), F32),
            pltpu.VMEM((GAIN_ROUNDS + 1, 1, D), F32),
            pltpu.VMEM((GAIN_ROUNDS, 1, D), F32),
            dma((8,)), dma((21,)),
            dma((16,)), dma((4,)),
            dma((60,)), dma((32,)), dma((4,)),
            dma((30,)), dma((2,)),
            dma((60,)), dma((1,)), dma((32,)),
            dma((1,)), dma((GAIN_ROUNDS,)),
        ],
        compiler_params=pltpu.CompilerParams(
            collective_id=0, has_side_effects=True, vmem_limit_bytes=46 * 2**20
        ),
        cost_estimate=pl.CostEstimate(
            flops=12 * ROWS * D * FF, bytes_accessed=22 * 2**20, transcendentals=2 * ROWS * FF
        ),
        name="mlp_block",
    )(tokens, layer_norm_gain.reshape(1, D), w_up, w_down, cotangent)
    mixed, grad_tokens, grad_up, grad_down, gain_grad = pl.pallas_call(
        store,
        out_shape=tuple(jax.ShapeDtypeStruct(shape, dtype) for shape, dtype in shapes),
        in_specs=[vmem] * 5,
        out_specs=(anywhere,) * 5,
        scratch_shapes=[dma((11,))],
        compiler_params=pltpu.CompilerParams(vmem_limit_bytes=2**20),
        cost_estimate=pl.CostEstimate(flops=0, bytes_accessed=10 * 2**20, transcendentals=0),
        name="store",
    )(*(pltpu.with_memory_space_constraint(one, pltpu.VMEM) for one in held))
    return mixed, grad_tokens, grad_up, grad_down, gain_grad.reshape(D)


def solution(mesh):
    placed = (P("dp", None), P(), P(None, "mp"), P("mp", None), P(("dp", "mp"), None))
    return jax.shard_map(
        shards,
        mesh=mesh,
        in_specs=placed,
        out_specs=(P(("dp", "mp"), None), P(("dp", "mp"), None), P(None, "mp"), P("mp", None), P()),
        check_vma=False,
    )
```
